256 devices in a mesh: row: 16 (over y, x_lo, core), col: 16 (over x_hi, z).
Axes of the slice: x: 4 (x_hi: 2, x_lo: 2; x = x_hi * 2 + x_lo), y: 4, z: 8, core: 2. Of those that a mesh axis runs over, the one named last changes fastest.
Arguments:
- feats: bfloat16 [32768, 2048], P(('row', 'col')), may hold values from -24 to 24
- weight: bfloat16 [2048, 512], replicated, may hold values from -0.125 to 0.125
- valid: int32 [32768], P(('row', 'col')), may hold values 0 or 1
Outputs:
- grad_embed: bfloat16 [32768, 512], P(('row', 'col'))
- grad_feats: bfloat16 [32768, 2048], P(('row', 'col'))
- grad_weight: float32 [2048, 512], P(('row', 'col'))
The draws below stay inside these ranges and needn't reach their ends.
All inputs are finite; a program needn't handle non-finite values. No bound on the sum of `valid` on one device may be relied on, other than what follows from the above.
Results may differ from the reference program's by a relative error of at most 0.028.
Values may be sent and summed in bfloat16 or wider, within the bound.
A program may use at most 64 MiB of HBM per device.

```python
import math
import jax
import jax.numpy as jnp
from jax import lax

FEAT = 2048
EMBED = 512
FRAMES = 32768
BAND = 128


def place_ends(array, own_key, least, largest):
    index_at = [jax.random.randint(jax.random.fold_in(own_key, axis), (), 0, length) for axis, length in enumerate(array.shape)]
    widest = array.shape.index(max(array.shape))
    beside = index_at[:widest] + [(index_at[widest] + 1) % array.shape[widest]] + index_at[widest + 1:]
    return array.at[tuple(index_at)].set(least).at[tuple(beside)].set(largest)


def spiked(array, key, source, target, shards_of, factor):
    def block_of(axis_at):
        return (jnp.arange(array.shape[axis_at]) // (array.shape[axis_at] // shards_of)).reshape((-1,) + (1,) * (array.ndim - 1 - axis_at))

    one_side = jax.random.permutation(key, shards_of)[block_of(target)]
    far = (block_of(target) + shards_of // 2) % shards_of
    return jnp.where((block_of(source) == one_side) | (block_of(source) == far), factor * array, array)


def levels(key, shape, cuts, low, largest):
    loudness, own = 1.0, jax.random.fold_in(key, 6)
    for position, blocks in cuts:
        heights = jnp.exp(jax.random.uniform(jax.random.fold_in(own, position), (blocks,), jnp.float32, low / len(cuts), largest / len(cuts)))
        loudness = loudness * jnp.repeat(heights, shape[position] // blocks).reshape([-1 if axis == position else 1 for axis in range(len(shape))])
    return loudness


def centred(key, dims, deviation, bound, cuts=(), kind=jnp.bfloat16):
    gain = levels(key, dims, cuts, -0.22, 0.18) if cuts else 1.0
    entries = jax.random.normal(key, dims, jnp.float32) * deviation * gain
    return jnp.minimum(jnp.maximum(entries, -bound), bound).astype(kind)


def heavy_noise(stream_key, extent, scale, limit, cuts, heavy, kind=jnp.bfloat16):
    entries = scale * jax.random.normal(stream_key, extent, jnp.float32)
    if cuts:
        entries = entries * levels(stream_key, extent, cuts, -0.22, 0.18)
    return jnp.clip(spiked(entries, jax.random.fold_in(stream_key, 3), *heavy), -limit, limit).astype(kind)


def setup_inputs(seed: int = 0) -> dict:
    key_list = jax.random.split(jax.random.key(seed), 4)
    return {
        "feats": heavy_noise(key_list[0], (FRAMES, FEAT), 1.0, 24.0, ((0, 256),), (0, 1, 256, 6.0)),
        "weight": centred(key_list[1], (FEAT, EMBED), FEAT ** -0.5, 0.125),
        "valid": place_ends((jax.random.randint(key_list[2], (FRAMES,), 0, 4) < 3).astype(jnp.int32), jax.random.fold_in(key_list[2], 1), 0, 1),
    }


def reference(feats, weight, valid):
    embedding = jnp.dot(feats, weight, preferred_element_type=jnp.float32).astype(jnp.bfloat16)
    wide = embedding.astype(jnp.float32)
    norm = lax.optimization_barrier(jnp.sum(wide * wide, axis=1))
    live = valid.astype(jnp.float32)
    width = math.gcd(FRAMES, 2048)
    count = FRAMES // width
    blocks = embedding.reshape(count, width, EMBED)
    norms = norm.reshape(count, width)

    def kernel(block, block_norm):
        inner = lax.dot_general(block, embedding, (((1,), (1,)), ((), ())), preferred_element_type=jnp.float32)
        return jnp.exp(-(block_norm[:, None] + norm[None, :] - 2.0 * inner) / jnp.float32(BAND))

    def mass_block(pieces):
        return lax.optimization_barrier(jnp.sum(kernel(pieces[0], pieces[1]) * live[None, :], axis=1))
    mass = lax.map(mass_block, (blocks, norms)).reshape(FRAMES) + 1.0 - live
    inverse = 1.0 / mass

    def pull_block(pieces):
        block, block_norm, block_inv = pieces
        pair = (live[None, :] * (block_inv[:, None] + inverse[None, :]) * kernel(block, block_norm)).astype(jnp.bfloat16)
        total = lax.optimization_barrier(jnp.sum(pair.astype(jnp.float32), axis=1))
        return block.astype(jnp.float32) * total[:, None] - jnp.dot(pair, embedding, preferred_element_type=jnp.float32)
    pull = lax.map(pull_block, (blocks, norms, inverse.reshape(count, width))).reshape(FRAMES, EMBED)
    grad_embed = (0.5 * live[:, None] * pull).astype(jnp.bfloat16)
    grad_feats = lax.dot_general(grad_embed, weight, (((1,), (1,)), ((), ())), preferred_element_type=jnp.float32).astype(jnp.bfloat16)
    grad_weight = lax.dot_general(feats, grad_embed, (((0,), (0,)), ((), ())), preferred_element_type=jnp.float32) * jnp.float32(math.sqrt(FEAT) / FRAMES)
    return (grad_embed, grad_feats, grad_weight)
```

```python
import functools
import math

import jax
import jax.numpy as jnp
from jax import lax
from jax.experimental import pallas as pl
from jax.experimental.pallas import tpu as pltpu
from jax.sharding import PartitionSpec as P

MESH = pl.DeviceIdType.MESH
XH, XL, Y, Z, C = 2, 2, 4, 8, 2
X = XH * XL
LINE = Z * C
PLANE = X * Y
FAR = 2.0**60


def device(x, y, z, k):
    return {"row": (y * XL + x % XL) * C + k, "col": (x // XL) * Z + z}


def to_row(column):
    n = column.shape[0]
    eye = lax.broadcasted_iota(jnp.int32, (n, n), 0) == lax.broadcasted_iota(jnp.int32, (n, n), 1)
    return jnp.sum(jnp.where(eye, column, 0.0), axis=0, keepdims=True)


def to_column(row):
    n = row.shape[1]
    eye = lax.broadcasted_iota(jnp.int32, (n, n), 0) == lax.broadcasted_iota(jnp.int32, (n, n), 1)
    return jnp.sum(jnp.where(eye, row, 0.0), axis=1, keepdims=True)


def nt(a, b):
    return lax.dot_general(a, b, (((1,), (1,)), ((), ())), preferred_element_type=jnp.float32)


def tn(a, b):
    return lax.dot_general(a, b, (((0,), (0,)), ((), ())), preferred_element_type=jnp.float32)


def kernel(
    feats, weight, valid,
    grad_embed, grad_feats, grad_weight,
    lines, planes, norms, tile, row_mass, row_masses, col_mass, col_masses,
    pulls, pulled, terms, term_in, parts, part_in,
    l_send, l_recv, q_send, q_recv, rm_send, rm_recv, cm_send, cm_recv,
    p_send, p_recv, t_send, t_recv, g_send, g_recv,
    *, band, scale,
):
    rows, embed = grad_embed.shape
    r, c = lax.axis_index("row"), lax.axis_index("col")
    k, x, y, z = r % C, (c // Z) * XL + (r // C) % XL, r // (C * XL), c % Z
    a = k * Z + z
    b = x * Y + y

    def line_mate(i):
        return device(x, y, i % Z, i // Z)

    def plane_mate(i):
        return device(i // Y, i % Y, z, k)

    barrier = pltpu.get_barrier_semaphore()

    def greet(d, carry):
        pl.semaphore_signal(barrier, inc=1, device_id=line_mate((a + d) % LINE), device_id_type=MESH)
        return carry

    def greet_plane(d, carry):
        pl.semaphore_signal(barrier, inc=1, device_id=plane_mate((b + d) % PLANE), device_id_type=MESH)
        return carry

    lax.fori_loop(1, LINE, greet, 0)
    lax.fori_loop(1, PLANE, greet_plane, 0)

    def at(ref, i, n):
        return ref.at[pl.ds(pl.multiple_of(i * n, n), n)]

    def copy(src, dst, send, recv, target):
        return pltpu.make_async_remote_copy(
            src_ref=src, dst_ref=dst, send_sem=send, recv_sem=recv, device_id=target, device_id_type=MESH
        )

    live_row = jnp.where(valid[...] > 0, 1.0, 0.0)
    live = to_column(live_row)
    embedding = jnp.dot(feats[...], weight[...], preferred_element_type=jnp.float32)
    away = jnp.where(lax.broadcasted_iota(jnp.int32, (rows, embed), 1) == 0, FAR, 0.0)
    own = jnp.where(live > 0.5, embedding, away).astype(jnp.bfloat16)
    at(lines, a, rows)[...] = own
    at(planes, b, rows)[...] = own

    pl.semaphore_wait(barrier, LINE + PLANE - 2)

    def line_copy(i, source):
        return copy(at(lines, a, rows), at(lines, source, rows), l_send.at[i], l_recv.at[source], line_mate(i))

    def plane_copy(i, source):
        return copy(at(planes, b, rows), at(planes, source, rows), q_send.at[i], q_recv.at[source], plane_mate(i))

    def over(n, me, action):
        def body(d, carry):
            action((me + d) % n)
            return carry

        lax.fori_loop(1, n, body, 0)

    over(LINE, a, lambda i: line_copy(i, a).start())
    over(PLANE, b, lambda i: plane_copy(i, b).start())
    over(LINE, a, lambda i: line_copy(i, i).wait_recv())
    over(PLANE, b, lambda i: plane_copy(i, i).wait_recv())

    def norm_step(i, carry):
        wide = at(planes, i, rows)[...].astype(jnp.float32)
        here = pl.ds(pl.multiple_of(i * rows, rows), rows)
        norms[0:1, here] = to_row(jnp.sum(wide * wide, axis=1, keepdims=True))
        return carry

    lax.fori_loop(0, PLANE, norm_step, 0)

    chunk = 2 * rows
    count = LINE // 2
    wide_columns = 512
    column_parts = PLANE * rows // wide_columns
    rate = -1.0 / (band * math.log(2.0))
    col_mass[...] = jnp.zeros_like(col_mass)

    def mass_step(i, carry):
        here = pl.ds(pl.multiple_of(i * chunk, chunk), chunk)
        block = lines[here, :]
        wide = block.astype(jnp.float32)
        norm = jnp.sum(wide * wide, axis=1, keepdims=True)
        twice = block * 2
        total = jnp.zeros((chunk, 1), jnp.float32)
        for j in range(column_parts):
            there = slice(j * wide_columns, (j + 1) * wide_columns)
            distance = (norm + norms[0:1, there]) - nt(twice, planes[there, :])
            value = jnp.exp2(distance * rate)
            tile[here, there] = value
            total = total + jnp.sum(value, axis=1, keepdims=True)
            col_mass[0:1, there] += jnp.sum(value, axis=0, keepdims=True)
        row_mass[pl.ds(i, 1), :] = to_row(total)
        return carry

    lax.fori_loop(0, count, mass_step, 0)

    def row_mass_copy(i, source):
        return copy(row_mass, row_masses.at[source], rm_send.at[i], rm_recv.at[source], line_mate(i))

    def col_mass_copy(i, source):
        return copy(col_mass, col_masses.at[source], cm_send.at[i], cm_recv.at[source], plane_mate(i))

    over(LINE, a, lambda i: row_mass_copy(i, a).start())
    over(PLANE, b, lambda i: col_mass_copy(i, b).start())
    row_masses[a] = row_mass[...]
    col_masses[b] = col_mass[...]
    over(LINE, a, lambda i: row_mass_copy(i, i).wait_recv())
    over(PLANE, b, lambda i: col_mass_copy(i, i).wait_recv())
    over(LINE, a, lambda i: row_mass_copy(i, i).wait_send())
    over(PLANE, b, lambda i: col_mass_copy(i, i).wait_send())
    row_mass[...] = 1.0 / jnp.sum(row_masses[...], axis=0)
    col_mass[...] = 1.0 / jnp.sum(col_masses[...], axis=0)

    def pull_copy(i, source):
        return copy(at(pulls, i, rows), at(pulled, source, rows), p_send.at[i], p_recv.at[source], line_mate(i))

    def pull_step(n, carry):
        i = (n + a // 2 + 1) % count
        here = pl.ds(pl.multiple_of(i * chunk, chunk), chunk)
        inverse = to_column(row_mass[pl.ds(i, 1), :])
        total = jnp.zeros((chunk, 1), jnp.float32)
        moved = jnp.zeros((chunk, embed), jnp.float32)
        for j in range(column_parts):
            there = slice(j * wide_columns, (j + 1) * wide_columns)
            pair = ((inverse + col_mass[0:1, there]) * tile[here, there]).astype(jnp.bfloat16)
            total = total + jnp.sum(pair.astype(jnp.float32), axis=1, keepdims=True)
            moved = moved + jnp.dot(pair, planes[there, :], preferred_element_type=jnp.float32)
        pulls[here, :] = (lines[here, :].astype(jnp.float32) * total - moved).astype(jnp.bfloat16)
        for m in range(2):

            @pl.when(2 * i + m != a)
            def _():
                pull_copy(2 * i + m, a).start()

        return carry

    lax.fori_loop(0, count, pull_step, 0)
    at(pulled, a, rows)[...] = at(pulls, a, rows)[...]
    over(LINE, a, lambda i: pull_copy(i, i).wait_recv())

    def add_pull(i, total):
        return total + at(pulled, i, rows)[...].astype(jnp.float32)

    pull = lax.fori_loop(0, LINE, add_pull, jnp.zeros((rows, embed), jnp.float32))
    gradient = jnp.where(live > 0.5, 0.5 * pull, 0.0).astype(jnp.bfloat16)
    grad_embed[...] = gradient

    natural = C * XH * Z * grad_weight.shape[0]
    share = Z * grad_weight.shape[0]
    for y_to in range(Y):
        for low in range(XL):
            start = (y_to * XL + low) * natural
            term = (tn(feats[:, start : start + natural], gradient) * scale).astype(jnp.bfloat16)
            for core in range(C):
                for high in range(XH):
                    to = (((high * XL + low) * Y + y_to) * C + core) * share
                    come = (core * XH + high) * share
                    terms[to : to + share, :] = term[come : come + share, :]
    slab = C * share

    def term_copy(i, source):
        return copy(at(terms, i, slab), at(term_in, source, slab), t_send.at[i], t_recv.at[source], plane_mate(i))

    over(PLANE, b, lambda i: term_copy(i, b).start())
    grad_feats[...] = nt(gradient, weight[...]).astype(jnp.bfloat16)
    at(term_in, b, slab)[...] = at(terms, b, slab)[...]
    over(PLANE, b, lambda i: term_copy(i, i).wait_recv())

    def add_term(i, total):
        return total + at(term_in, i, slab)[...].astype(jnp.float32)

    summed = lax.fori_loop(0, PLANE, add_term, jnp.zeros((slab, embed), jnp.float32))
    for i in range(LINE):
        parts[i] = summed[i * (slab // LINE) : (i + 1) * (slab // LINE), :]

    def part_copy(i, source):
        return copy(parts.at[i], part_in.at[source], g_send.at[i], g_recv.at[source], line_mate(i))

    over(LINE, a, lambda i: part_copy(i, a).start())
    part_in[a] = parts[a]
    over(LINE, a, lambda i: part_copy(i, i).wait_recv())
    grad_weight[...] = jnp.sum(part_in[...], axis=0)

    over(LINE, a, lambda i: line_copy(i, i).wait_send())
    over(PLANE, b, lambda i: plane_copy(i, i).wait_send())
    over(LINE, a, lambda i: pull_copy(i, i).wait_send())
    over(PLANE, b, lambda i: term_copy(i, i).wait_send())
    over(LINE, a, lambda i: part_copy(i, i).wait_send())


def local(feats, weight, valid):
    rows, width = feats.shape
    embed = weight.shape[1]
    devices = LINE * PLANE
    frames = rows * devices
    out_rows = width // devices
    half, single = jnp.bfloat16, jnp.float32
    vmem = pl.BlockSpec(memory_space=pltpu.VMEM)
    dma = pltpu.SemaphoreType.DMA
    return pl.pallas_call(
        functools.partial(
            kernel, band=float(embed // 4), scale=math.sqrt(width) / frames
        ),
        out_shape=(
            jax.ShapeDtypeStruct((rows, embed), half),
            jax.ShapeDtypeStruct((rows, width), half),
            jax.ShapeDtypeStruct((out_rows, embed), single),
        ),
        in_specs=[vmem] * 3,
        out_specs=(vmem,) * 3,
        scratch_shapes=[
            pltpu.VMEM((LINE * rows, embed), half),
            pltpu.VMEM((PLANE * rows, embed), half),
            pltpu.VMEM((1, PLANE * rows), single),
            pltpu.VMEM((LINE * rows, PLANE * rows), single),
            pltpu.VMEM((LINE // 2, 2 * rows), single),
            pltpu.VMEM((LINE, LINE // 2, 2 * rows), single),
            pltpu.VMEM((1, PLANE * rows), single),
            pltpu.VMEM((PLANE, 1, PLANE * rows), single),
            pltpu.VMEM((LINE * rows, embed), half),
            pltpu.VMEM((LINE * rows, embed), half),
            pltpu.VMEM((width, embed), half),
            pltpu.VMEM((width, embed), half),
            pltpu.VMEM((LINE, out_rows, embed), single),
            pltpu.VMEM((LINE, out_rows, embed), single),
        ]
        + [dma((LINE,)), dma((LINE,)), dma((PLANE,)), dma((PLANE,))] * 2
        + [dma((LINE,)), dma((LINE,)), dma((PLANE,)), dma((PLANE,)), dma((LINE,)), dma((LINE,))],
        compiler_params=pltpu.CompilerParams(
            collective_id=0, has_side_effects=True, vmem_limit_bytes=56 * 1024 * 1024
        ),
    )(feats, weight, valid.reshape(1, rows))


def solution(mesh):
    spec = P(("row", "col"), None)
    return jax.shard_map(
        local,
        mesh=mesh,
        in_specs=(spec, P(), P(("row", "col"))),
        out_specs=(spec, spec, spec),
        check_vma=False,
    )
```

```python
import functools
import math

import jax
import jax.numpy as jnp
from jax import lax
from jax.experimental import pallas as pl
from jax.experimental.pallas import tpu as pltpu
from jax.sharding import PartitionSpec as P

MESH = pl.DeviceIdType.MESH
XH, XL, Y, Z, C = 2, 2, 4, 8, 2
X = XH * XL
LINE = Z * C
PLANE = X * Y
FAR = 2.0**60
HALF, SINGLE = jnp.bfloat16, jnp.float32


def device(x, y, z, k):
    return {"row": (y * XL + x % XL) * C + k, "col": (x // XL) * Z + z}


def to_row(column):
    n = column.shape[0]
    eye = lax.broadcasted_iota(jnp.int32, (n, n), 0) == lax.broadcasted_iota(jnp.int32, (n, n), 1)
    return jnp.sum(jnp.where(eye, column, 0.0), axis=0, keepdims=True)


def to_column(row):
    n = row.shape[1]
    eye = lax.broadcasted_iota(jnp.int32, (n, n), 0) == lax.broadcasted_iota(jnp.int32, (n, n), 1)
    return jnp.sum(jnp.where(eye, row, 0.0), axis=1, keepdims=True)


def nt(a, b):
    return lax.dot_general(a, b, (((1,), (1,)), ((), ())), preferred_element_type=SINGLE)


def tn(a, b):
    return lax.dot_general(a, b, (((0,), (0,)), ((), ())), preferred_element_type=SINGLE)


class Gather:
    def __init__(self, send, recv):
        self.send, self.recv = send, recv
        self.made, self.arrived = {}, set()

    def add(self, name, make, needs=()):
        number = len(self.made)
        self.made[name] = (lambda mine: make(mine, self.send.at[number], self.recv.at[number])), needs

    def start(self, *names):
        for name in names:
            make, needs = self.made[name]
            for need in needs:
                self.wait(need)
            make(True).start()

    def wait(self, *names):
        for name in names:
            if name not in self.arrived:
                self.arrived.add(name)
                self.made[name][0](False).wait_recv()

    def finish(self):
        for name in self.made:
            self.made[name][0](True).wait_send()


def kernel(
    feats, weight, valid,
    grad_embed, grad_feats, grad_weight,
    lines, planes, norms, tile, row_mass, row_in, row_pair, row_ins, col_mass, col_ins, col_part, col_ins2,
    mine, sib_out, sib_in, run_out, run_in,
    mixed, leaving, gradients, first_out, first_in, second_out, second_in, third_out, third_in,
    g_send, g_recv, m_send, m_recv, s_send, s_recv, r_send, r_recv, w_send, w_recv,
    *, band, scale,
):
    rows, embed = grad_embed.shape
    r, c = lax.axis_index("row"), lax.axis_index("col")
    k, x, y, z = r % C, (c // Z) * XL + (r // C) % XL, r // (C * XL), c % Z
    sibling = device(x, y, z, 1 - k)

    def z_mate(d):
        return device(x, y, (z + d + Z) % Z, k)

    def x_mate(d):
        return device((x + d + X) % X, y, z, k)

    def y_mate(d):
        return device(x, (y + d + Y) % Y, z, k)

    barrier = pltpu.get_barrier_semaphore()
    friends = [sibling] + [z_mate(d) for d in range(1, Z)]
    friends += [x_mate(d) for d in range(1, X)] + [y_mate(d) for d in range(1, Y)]
    for friend in friends:
        pl.semaphore_signal(barrier, inc=1, device_id=friend, device_id_type=MESH)

    def span(start, n):
        return pl.ds(pl.multiple_of(start, n), n)

    def copy(src, dst, send, recv, target):
        return pltpu.make_async_remote_copy(
            src_ref=src, dst_ref=dst, send_sem=send, recv_sem=recv, device_id=target, device_id_type=MESH
        )

    live = to_column(jnp.where(valid[...] > 0, 1.0, 0.0))
    embedding = jnp.dot(feats[...], weight[...], preferred_element_type=SINGLE)
    away = jnp.where(lax.broadcasted_iota(jnp.int32, (rows, embed), 1) == 0, FAR, 0.0)
    own = jnp.where(live > 0.5, embedding, away).astype(HALF)
    lines[span((z * C + k) * rows, rows), :] = own
    planes[span((y * X + x) * rows, rows), :] = own
    group = XH * Z * grad_weight.shape[0]
    for g in range(Y * XL):
        low, high = feats[:, 2 * g * group : (2 * g + 1) * group], feats[:, (2 * g + 1) * group : (2 * g + 2) * group]
        here = slice(g * group, (g + 1) * group)
        mixed[0:rows, here] = jnp.where(k == 0, low, high)
        leaving[:, here] = jnp.where(k == 0, high, low)

    pl.semaphore_wait(barrier, len(friends))

    half, quarter = rows // 2, rows // 4
    gather = Gather(g_send, g_recv)

    def line_at(dz, core, start, n):
        return lines.at[span(((z + dz + Z) % Z * C + core) * rows + start, n)]

    def plane_at(dx, dy, start, n):
        return planes.at[span(((y + dy + Y) % Y * X + (x + dx + X) % X) * rows + start, n)]

    def along_z(s, d, h):
        def make(sender, send, recv):
            from_here = -s * (d - 1) if sender else -s * d
            ref = line_at(from_here, k, h * half, half)
            return copy(ref, ref, send, recv, z_mate(s))

        return make

    for s in (1, -1):
        for d in range(1, Z // 2 + 1):
            for h in (0, 1):
                if d < Z // 2 or h == (0 if s == 1 else 1):
                    gather.add(("z", s, d, h), along_z(s, d, h), [("z", s, d - 1, h)] if d > 1 else [])

    def across(o):
        def make(sender, send, recv):
            ref = line_at(o, k if sender else 1 - k, 0, rows)
            return copy(ref, ref, send, recv, sibling)

        return make

    for o in range(-Z // 2 + 1, Z // 2 + 1):
        if o == 0:
            needs = []
        elif o == Z // 2:
            needs = [("z", 1, o, 0), ("z", -1, o, 1)]
        else:
            needs = [("z", -1 if o > 0 else 1, abs(o), h) for h in (0, 1)]
        gather.add(("c", o), across(o), needs)

    def in_plane(axis, s, along, beside, start, n):
        def make(sender, send, recv):
            o = along if sender else along - s
            ref = plane_at(o, beside, start, n) if axis == "x" else plane_at(beside, o, start, n)
            return copy(ref, ref, send, recv, x_mate(s) if axis == "x" else y_mate(s))

        return make

    for axis, other, h in (("y", "x", 0), ("x", "y", 1)):
        for s in (1, -1):
            part = 0 if s == 1 else 1
            for g in (0, 1):
                gather.add((axis, s, "own", g), in_plane(axis, s, 0, 0, g * half, half))
            gather.add((axis, s, "far"), in_plane(axis, s, -s, 0, part * half, half), [(axis, s, "own", part)])
            for t in (1, -1):
                gather.add((axis, s, "side", t), in_plane(axis, s, 0, t, h * half, half), [(other, -t, "own", h)])
                gather.add(
                    (axis, s, "side far", t),
                    in_plane(axis, s, -s, t, h * half + part * quarter, quarter),
                    [(axis, s, "side", t)],
                )
            gather.add(
                (axis, s, "across"),
                in_plane(axis, s, 0, 2, h * half, half),
                [(other, 1 if h == 0 else -1, "far")],
            )
            gather.add(
                (axis, s, "across far"),
                in_plane(axis, s, -s, 2, h * half + part * quarter, quarter),
                [(axis, s, "across")],
            )

    def swap_copy(mine_, send, recv):
        return copy(leaving, mixed.at[span(rows, rows)], send, recv, sibling)

    gather.add("feats", swap_copy)

    both = (1, -1)
    gather.start(*[("x", s, "own", 0) for s in both], *[("y", s, "own", 1) for s in both])
    gather.start(*[("z", s, 1, 0) for s in both])
    gather.start(*[("x", s, "own", 1) for s in both], *[("y", s, "own", 0) for s in both])
    gather.start(*[("z", s, 1, 1) for s in both], ("c", 0), "feats")

    def norm_of(*offsets):
        for dx, dy in offsets:
            place = ((y + dy + Y) % Y * X + (x + dx + X) % X) * rows
            wide = planes[span(place, rows), :].astype(SINGLE)
            norms[0:1, span(place, rows)] = to_row(jnp.sum(wide * wide, axis=1, keepdims=True))

    norm_of((0, 0))
    gather.start(*[("z", s, 2, 0) for s in both], ("x", 1, "far"), ("y", -1, "far"))
    gather.start(*[(axis, s, "side", t) for t in both for axis in "yx" for s in both])
    gather.start(*[("z", s, 2, 1) for s in both], ("x", -1, "far"), ("y", 1, "far"), ("c", 1), ("c", -1))
    gather.wait(*[(axis, s, "own", g) for axis in "xy" for s in both for g in (0, 1)])
    norm_of((1, 0), (-1, 0), (0, 1), (0, -1))
    gather.start(*[("z", s, 3, 0) for s in both])
    gather.start(*[(axis, s, "across") for axis in "yx" for s in both])
    gather.start(*[(axis, s, "side far", t) for t in both for axis in "yx" for s in both])
    gather.start(*[("z", s, 3, 1) for s in both], ("c", 2), ("c", -2))
    gather.start(("z", 1, 4, 0), ("z", -1, 4, 1))
    gather.start(*[(axis, s, "across far") for axis in "yx" for s in both])
    gather.wait(*[(axis, s, "side", t) for axis in "xy" for s in both for t in both])
    gather.wait(*[(axis, s, "far") for axis in "xy" for s in both])
    norm_of((1, 1), (1, -1), (-1, 1), (-1, -1), (2, 0), (0, 2))
    gather.start(("c", 3), ("c", -3), ("c", 4))
    gather.wait(*gather.made)
    norm_of((2, 1), (2, -1), (1, 2), (-1, 2), (2, 2))

    chunk = C * rows
    tall, wide_columns = 2 * chunk, chunk
    rate = -1.0 / (band * math.log(2.0))
    col_mass[...] = jnp.zeros_like(col_mass)

    def mass_step(i, carry):
        here = span(i * tall, tall)
        block = lines[here, :]
        wide = block.astype(SINGLE)
        norm = jnp.sum(wide * wide, axis=1, keepdims=True)
        twice = block * 2
        total = jnp.zeros((tall, 1), SINGLE)
        for j in range(PLANE * rows // wide_columns):
            there = slice(j * wide_columns, (j + 1) * wide_columns)
            distance = (norm + norms[0:1, there]) - nt(twice, planes[there, :])
            value = jnp.exp2(distance * rate)
            tile[here, there] = value
            total = total + jnp.sum(value, axis=1, keepdims=True)
            col_mass[0:1, there] += jnp.sum(value, axis=0, keepdims=True)
        for j in range(2):
            row_mass[pl.ds(2 * i + j, 1), :] = to_row(total[j * chunk : (j + 1) * chunk, :])
        return carry

    lax.fori_loop(0, Z // 2, mass_step, 0)

    mass = Gather(m_send, m_recv)
    mass.add("c", lambda mine_, send, recv: copy(row_mass, row_in, send, recv, sibling))

    def direct(source, target, mate, size, at, d):
        def make(sender, send, recv):
            return copy(source, target.at[at if sender else (at - d + size) % size], send, recv, mate(d))

        return make

    for d in range(1, X):
        mass.add(("x", d), direct(col_mass, col_ins, x_mate, X, x, d))
    for d in range(1, Y):
        mass.add(("y", d), direct(col_part, col_ins2, y_mate, Y, y, d))
    for d in range(1, Z):
        mass.add(("z", d), direct(row_pair, row_ins, z_mate, Z, z, d))
    mass.start("c", *[("x", d) for d in range(1, X)])
    col_ins[x] = col_mass[...]
    mass.wait("c")
    row_pair[...] = row_mass[...] + row_in[...]
    mass.start(*[("z", d) for d in range(1, Z)])
    row_ins[z] = row_pair[...]
    mass.wait(*[("x", d) for d in range(1, X)])
    col_part[...] = jnp.sum(col_ins[...], axis=0)
    mass.start(*[("y", d) for d in range(1, Y)])
    col_ins2[y] = col_part[...]
    mass.wait(*mass.made)
    mass.finish()
    row_mass[...] = 1.0 / jnp.sum(row_ins[...], axis=0)
    col_mass[...] = 1.0 / jnp.sum(col_ins2[...], axis=0)

    def pair_copy(n):
        return copy(sib_out.at[n], sib_in.at[n], s_send.at[n], s_recv.at[n], sibling)

    def run_copy(s, m, h):
        here = pl.ds(h * half, half)
        at = (s * 4 + m) * 2 + h
        return copy(
            run_out.at[s * 4 + m, here], run_in.at[s * 4 + m, here], r_send.at[at], r_recv.at[at], z_mate(2 * s - 1)
        )

    run_in[4, half:rows, :] = jnp.zeros((half, embed), HALF)
    run_in[0, 0:half, :] = jnp.zeros((half, embed), HALF)

    def link(i):
        m, s = (i + 1) // 2, i % 2
        pair_copy(i).wait_recv()
        for h in (0, 1):
            here = slice(h * half, (h + 1) * half)

            @pl.when(jnp.logical_or(m > 1, s == 1 - h))
            def _():
                run_copy(s, m - 1, h).wait_recv()

            total = mine[i, here, :] + sib_in[i, here, :].astype(SINGLE) + run_in[s * 4 + m - 1, here, :].astype(SINGLE)
            run_out[s * 4 + m, here, :] = total.astype(HALF)
            run_copy(s, m, h).start()

    def pull_step(n, carry):
        o = (4 - (n + 1) // 2) * (2 * (n % 2) - 1)
        i = (z + o + Z) % Z
        here = span(i * chunk, chunk)
        inverse = to_column(row_mass[pl.ds(i, 1), :])
        total = jnp.zeros((chunk, 1), SINGLE)
        moved = jnp.zeros((chunk, embed), SINGLE)
        width = 2 * chunk
        for j in range(PLANE * rows // width):
            there = slice(j * width, (j + 1) * width)
            pair = ((inverse + col_mass[0:1, there]) * tile[here, there]).astype(HALF)
            total = total + jnp.sum(pair.astype(SINGLE), axis=1, keepdims=True)
            moved = moved + jnp.dot(pair, planes[there, :], preferred_element_type=SINGLE)
        pull = lines[here, :].astype(SINGLE) * total - moved
        mine[n] = jnp.where(k == 0, pull[0:rows, :], pull[rows:chunk, :])
        sib_out[n] = jnp.where(k == 0, pull[rows:chunk, :], pull[0:rows, :]).astype(HALF)
        pair_copy(n).start()

        @pl.when(n == 1)
        def _():
            pair_copy(0).wait_recv()
            far = (mine[0] + sib_in[0].astype(SINGLE)).astype(HALF)
            run_out[4] = far
            run_out[0] = far
            run_copy(1, 0, 0).start()
            run_copy(0, 0, 1).start()

        @pl.when(n >= 2)
        def _():
            link(n - 1)

        return carry

    lax.fori_loop(0, Z, pull_step, 0)
    pair_copy(Z - 1).wait_recv()
    pull = mine[Z - 1] + sib_in[Z - 1].astype(SINGLE)
    for s in (0, 1):
        for h in (0, 1):
            run_copy(s, 3, h).wait_recv()
        pull = pull + run_in[s * 4 + 3].astype(SINGLE)
    gradient = jnp.where(live > 0.5, 0.5 * pull, 0.0).astype(HALF)

    gradients[0:rows, :] = gradient
    terms = Gather(w_send, w_recv)
    terms.add("c", lambda mine_, send, recv: copy(gradients.at[span(0, rows)], gradients.at[span(rows, rows)], send, recv, sibling))
    terms.start("c")
    grad_embed[...] = gradient
    gather.wait("feats")
    split = embed // 2
    share = group // XH

    def first(table, axis, mate, size, at, d):
        def make(sender, send, recv):
            return copy(
                first_out.at[table, (at + d) % size],
                first_in.at[table, at if sender else (at - d + size) % size],
                send, recv, mate(d),
            )

        return make

    def second(table, mate, size, at, d):
        def make(sender, send, recv):
            return copy(
                second_out.at[table, (at + d) % size],
                second_in.at[table, at if sender else (at - d + size) % size],
                send, recv, mate(d),
            )

        return make

    def third(d):
        def make(sender, send, recv):
            return copy(third_out.at[(z + d) % Z], third_in.at[z if sender else (z - d + Z) % Z], send, recv, z_mate(d))

        return make

    for d in range(1, X):
        terms.add(("first", 0, d), first(0, "x", x_mate, X, x, d))
        terms.add(("second", 1, d), second(1, x_mate, X, x, d))
    for d in range(1, Y):
        terms.add(("first", 1, d), first(1, "y", y_mate, Y, y, d))
        terms.add(("second", 0, d), second(0, y_mate, Y, y, d))
    for d in range(1, Z):
        terms.add(("third", d), third(d))

    terms.wait("c")
    both_gradients = gradients[...]
    for g in range(Y * XL):
        to_y, low = g // XL, g % XL
        term = (tn(mixed[:, g * group : (g + 1) * group], both_gradients) * scale).astype(HALF)
        for high in range(XH):
            to_x = high * XL + low
            piece = term[high * share : (high + 1) * share, :]
            first_out[0, to_x, to_y * share : (to_y + 1) * share, :] = piece[:, 0:split]
            first_out[1, to_y, to_x * share : (to_x + 1) * share, :] = piece[:, split:embed]
    for d in range(1, X):
        terms.start(("first", 0, d), ("first", 1, d))
    grad_feats[...] = nt(gradient, weight[...]).astype(HALF)
    for table, at in ((0, x), (1, y)):
        first_in[table, at] = first_out[table, at]
        terms.wait(*[("first", table, d) for d in range(1, X)])
        added = jnp.sum(first_in[table].astype(SINGLE), axis=0).astype(HALF)
        for i in range(4):
            second_out[table, i] = added[i * share : (i + 1) * share, :]
        terms.start(*[("second", table, d) for d in range(1, X)])
    for table, at in ((0, y), (1, x)):
        second_in[table, at] = second_out[table, at]
        terms.wait(*[("second", table, d) for d in range(1, X)])
        added = jnp.sum(second_in[table].astype(SINGLE), axis=0)
        for i in range(Z):
            third_out[i, :, table * split : (table + 1) * split] = added[i * (share // Z) : (i + 1) * (share // Z), :]
    terms.start(*[("third", d) for d in range(1, Z)])
    third_in[z] = third_out[z]
    terms.wait(*terms.made)
    grad_weight[...] = jnp.sum(third_in[...], axis=0)

    gather.finish()
    terms.finish()
    for n in range(Z):
        pair_copy(n).wait_send()
    run_copy(1, 0, 0).wait_send()
    run_copy(0, 0, 1).wait_send()
    for s in (0, 1):
        for m in (1, 2, 3):
            for h in (0, 1):
                run_copy(s, m, h).wait_send()


def local(feats, weight, valid):
    rows, width = feats.shape
    embed = weight.shape[1]
    frames = rows * LINE * PLANE
    out_rows = width // (LINE * PLANE)
    vmem = pl.BlockSpec(memory_space=pltpu.VMEM)

    def half(*shape):
        return pltpu.VMEM(shape, HALF)

    def single(*shape):
        return pltpu.VMEM(shape, SINGLE)

    def dma(n):
        return [pltpu.SemaphoreType.DMA((n,))] * 2

    share = Z * out_rows
    columns = PLANE * rows
    return pl.pallas_call(
        functools.partial(kernel, band=float(embed // 4), scale=math.sqrt(width) / frames),
        out_shape=(
            jax.ShapeDtypeStruct((rows, embed), HALF),
            jax.ShapeDtypeStruct((rows, width), HALF),
            jax.ShapeDtypeStruct((out_rows, embed), SINGLE),
        ),
        in_specs=[vmem] * 3,
        out_specs=(vmem,) * 3,
        scratch_shapes=[
            half(LINE * rows, embed), half(columns, embed), single(1, columns), single(LINE * rows, columns),
            single(Z, C * rows), single(Z, C * rows), single(Z, C * rows), single(Z, Z, C * rows),
            single(1, columns), single(X, 1, columns), single(1, columns), single(Y, 1, columns),
            single(Z, rows, embed), half(Z, rows, embed), half(Z, rows, embed),
            half(8, rows, embed), half(8, rows, embed),
            half(2 * rows, width // 2), half(rows, width // 2), half(2 * rows, embed),
            half(2, 4, 4 * share, embed // 2), half(2, 4, 4 * share, embed // 2),
            half(2, 4, share, embed // 2), half(2, 4, share, embed // 2),
            single(Z, out_rows, embed), single(Z, out_rows, embed),
        ]
        + dma(64) + dma(14) + dma(Z) + dma(16) + dma(20),
        compiler_params=pltpu.CompilerParams(
            collective_id=0, has_side_effects=True, vmem_limit_bytes=56 * 1024 * 1024
        ),
    )(feats, weight, valid.reshape(1, rows))


def solution(mesh):
    spec = P(("row", "col"), None)
    return jax.shard_map(
        local,
        mesh=mesh,
        in_specs=(spec, P(), P(("row", "col"))),
        out_specs=(spec, spec, spec),
        check_vma=False,
    )
```

```python
import functools
import math

import jax
import jax.numpy as jnp
from jax import lax
from jax.experimental import pallas as pl
from jax.experimental.pallas import tpu as pltpu
from jax.sharding import PartitionSpec as P

MESH = pl.DeviceIdType.MESH
XH, XL, Y, Z, C = 2, 2, 4, 8, 2
X = XH * XL
LINE = Z * C
PLANE = X * Y
FAR = 2.0**60
ALONG = (0, 1, -1, 2, -2, 3, -3, 4)
AROUND = (
    (0, 0), (1, 0), (-1, 0), (0, 1), (0, -1), (2, 0), (0, 2), (1, 1), (-1, 1), (1, -1), (-1, -1),
    (2, 1), (2, -1), (1, 2), (-1, 2), (2, 2),
)
HALF, SINGLE = jnp.bfloat16, jnp.float32


def line_slot(dz):
    return ALONG.index((dz + Z // 2 - 1) % Z - Z // 2 + 1)


def plane_slot(dx, dy):
    return AROUND.index(((dx + 1) % X - 1, (dy + 1) % Y - 1))


def device(x, y, z, k):
    return {"row": (y * XL + x % XL) * C + k, "col": (x // XL) * Z + z}


def to_row(column):
    n = column.shape[0]
    eye = lax.broadcasted_iota(jnp.int32, (n, n), 0) == lax.broadcasted_iota(jnp.int32, (n, n), 1)
    return jnp.sum(jnp.where(eye, column, 0.0), axis=0, keepdims=True)


def to_column(row):
    n = row.shape[1]
    eye = lax.broadcasted_iota(jnp.int32, (n, n), 0) == lax.broadcasted_iota(jnp.int32, (n, n), 1)
    return jnp.sum(jnp.where(eye, row, 0.0), axis=1, keepdims=True)


def nt(a, b):
    return lax.dot_general(a, b, (((1,), (1,)), ((), ())), preferred_element_type=SINGLE)


def tn(a, b):
    return lax.dot_general(a, b, (((0,), (0,)), ((), ())), preferred_element_type=SINGLE)


class Gather:
    def __init__(self, send, recv):
        self.send, self.recv = send, recv
        self.made, self.arrived = {}, set()

    def add(self, name, make, needs=()):
        number = len(self.made)
        self.made[name] = (lambda mine: make(mine, self.send.at[number], self.recv.at[number])), needs

    def start(self, *names):
        for name in names:
            make, needs = self.made[name]
            for need in needs:
                self.wait(need)
            make(True).start()

    def wait(self, *names):
        for name in names:
            if name not in self.arrived:
                self.arrived.add(name)
                self.made[name][0](False).wait_recv()

    def finish(self):
        for name in self.made:
            self.made[name][0](True).wait_send()


def kernel(
    feats_in, weight_in, valid_in,
    grad_embed, grad_feats, grad_weight,
    feats, weight, valid, embed_out, feats_out, weight_out,
    lines, planes, norms, tile, row_norm, row_sum, col_sum,
    row_mass, row_in, row_pair, row_ins, col_mass, col_ins, col_part, col_ins2,
    mine, sib_out, sib_in, run_out, run_in,
    mixed, leaving, gradients, first_out, first_in, second_out, second_in, third_out, third_in,
    load, store, g_send, g_recv, m_send, m_recv, s_send, s_recv, r_send, r_recv, w_send, w_recv,
    *, band, scale,
):
    rows, embed = grad_embed.shape
    r, c = lax.axis_index("row"), lax.axis_index("col")
    k, x, y, z = r % C, (c // Z) * XL + (r // C) % XL, r // (C * XL), c % Z
    sibling = device(x, y, z, 1 - k)

    def z_mate(d):
        return device(x, y, (z + d + Z) % Z, k)

    def x_mate(d):
        return device((x + d + X) % X, y, z, k)

    def y_mate(d):
        return device(x, (y + d + Y) % Y, z, k)

    barrier = pltpu.get_barrier_semaphore()
    friends = [sibling] + [z_mate(d) for d in range(1, Z)]
    friends += [x_mate(d) for d in range(1, X)] + [y_mate(d) for d in range(1, Y)]
    for friend in friends:
        pl.semaphore_signal(barrier, inc=1, device_id=friend, device_id_type=MESH)

    depth = weight.shape[0] // 4
    loads = [
        pltpu.make_async_copy(valid_in, valid, load.at[0]),
        pltpu.make_async_copy(feats_in, feats, load.at[1]),
    ]
    for i in range(4):
        part = pl.ds(i * depth, depth)
        loads.append(pltpu.make_async_copy(weight_in.at[part], weight.at[part], load.at[2 + i]))
    for one in loads:
        one.start()
    col_sum[...] = jnp.zeros_like(col_sum)
    loads[0].wait()
    loads[1].wait()

    def span(start, n):
        return pl.ds(pl.multiple_of(start, n), n)

    def copy(src, dst, send, recv, target):
        return pltpu.make_async_remote_copy(
            src_ref=src, dst_ref=dst, send_sem=send, recv_sem=recv, device_id=target, device_id_type=MESH
        )

    live = to_column(jnp.where(valid[...] > 0, 1.0, 0.0))
    embedding = jnp.zeros((rows, embed), SINGLE)
    for i in range(4):
        loads[2 + i].wait()
        part = slice(i * depth, (i + 1) * depth)
        embedding = embedding + jnp.dot(feats[:, part], weight[part, :], preferred_element_type=SINGLE)
    away = jnp.where(lax.broadcasted_iota(jnp.int32, (rows, embed), 1) == 0, FAR, 0.0)
    own = jnp.where(live > 0.5, embedding, away).astype(HALF)
    lines[span(k * rows, rows), :] = own
    planes[0:rows, :] = own
    group = XH * Z * grad_weight.shape[0]
    for g in range(Y * XL):
        low, high = feats[:, 2 * g * group : (2 * g + 1) * group], feats[:, (2 * g + 1) * group : (2 * g + 2) * group]
        here = slice(g * group, (g + 1) * group)
        mixed[0:rows, here] = jnp.where(k == 0, low, high)
        leaving[:, here] = jnp.where(k == 0, high, low)

    pl.semaphore_wait(barrier, len(friends))

    half, quarter = rows // 2, rows // 4
    gather = Gather(g_send, g_recv)

    def line_at(dz, core, start, n):
        return lines.at[span((line_slot(dz) * C + core) * rows + start, n)]

    def plane_at(dx, dy, start, n):
        return planes.at[pl.ds(plane_slot(dx, dy) * rows + start, n)]

    def along_z(s, d, h):
        def make(sender, send, recv):
            source = line_at(-s * (d - 1), k, h * half, half)
            return copy(source, line_at(-s * d, k, h * half, half), send, recv, z_mate(s))

        return make

    for s in (1, -1):
        for d in range(1, Z // 2 + 1):
            for h in (0, 1):
                if d < Z // 2 or h == (0 if s == 1 else 1):
                    gather.add(("z", s, d, h), along_z(s, d, h), [("z", s, d - 1, h)] if d > 1 else [])

    def across(o):
        def make(sender, send, recv):
            ref = line_at(o, k if sender else 1 - k, 0, rows)
            return copy(ref, ref, send, recv, sibling)

        return make

    for o in range(-Z // 2 + 1, Z // 2 + 1):
        if o == 0:
            needs = []
        elif o == Z // 2:
            needs = [("z", 1, o, 0), ("z", -1, o, 1)]
        else:
            needs = [("z", -1 if o > 0 else 1, abs(o), h) for h in (0, 1)]
        gather.add(("c", o), across(o), needs)

    def in_plane(axis, s, along, beside, start, n):
        def make(sender, send, recv):
            if axis == "x":
                source, target = plane_at(along, beside, start, n), plane_at(along - s, beside, start, n)
                return copy(source, target, send, recv, x_mate(s))
            source, target = plane_at(beside, along, start, n), plane_at(beside, along - s, start, n)
            return copy(source, target, send, recv, y_mate(s))

        return make

    for axis, other, h in (("y", "x", 0), ("x", "y", 1)):
        for s in (1, -1):
            part = 0 if s == 1 else 1
            for g in (0, 1):
                gather.add((axis, s, "own", g), in_plane(axis, s, 0, 0, g * half, half))
            gather.add((axis, s, "far"), in_plane(axis, s, -s, 0, part * half, half), [(axis, s, "own", part)])
            for t in (1, -1):
                gather.add((axis, s, "side", t), in_plane(axis, s, 0, t, h * half, half), [(other, -t, "own", h)])
                gather.add(
                    (axis, s, "side far", t),
                    in_plane(axis, s, -s, t, h * half + part * quarter, quarter),
                    [(axis, s, "side", t)],
                )
            gather.add(
                (axis, s, "across"),
                in_plane(axis, s, 0, 2, h * half, half),
                [(other, 1 if h == 0 else -1, "far")],
            )
            gather.add(
                (axis, s, "across far"),
                in_plane(axis, s, -s, 2, h * half + part * quarter, quarter),
                [(axis, s, "across")],
            )

    def swap_copy(mine_, send, recv):
        return copy(leaving, mixed.at[span(rows, rows)], send, recv, sibling)

    gather.add("feats", swap_copy)

    both = (1, -1)
    gather.start(*[("x", s, "own", 0) for s in both], *[("y", s, "own", 1) for s in both])
    gather.start(*[("z", s, 1, 0) for s in both])
    gather.start(*[("x", s, "own", 1) for s in both], *[("y", s, "own", 0) for s in both])
    gather.start(*[("z", s, 1, 1) for s in both], ("c", 0), "feats")

    def norm_of(first, last):
        for i in range(first, last):
            here = slice(i * rows, (i + 1) * rows)
            wide = planes[here, :].astype(SINGLE)
            norms[0:1, here] = to_row(jnp.sum(wide * wide, axis=1, keepdims=True))

    chunk = C * rows
    rate = -1.0 / (band * math.log(2.0))

    def work(first_row, last_row, first_unit, last_unit):
        def step(i, carry):
            here = span(i * chunk, chunk)
            block = lines[here, :]
            if first_unit == 0:
                wide = block.astype(SINGLE)
                norm = jnp.broadcast_to(jnp.sum(wide * wide, axis=1, keepdims=True), (chunk, 128))
                row_norm[here, :] = norm
                total = jnp.zeros((chunk, 128), SINGLE)
            else:
                norm = row_norm[here, :]
                total = row_sum[here, :]
            norm = jnp.concatenate([norm] * (chunk // 128), axis=1)
            twice = block * 2
            for j in range(first_unit, last_unit):
                there = slice(j * chunk, (j + 1) * chunk)
                distance = (norm + norms[0:1, there]) - nt(twice, planes[there, :])
                value = jnp.exp2(distance * rate)
                tile[here, there] = value
                for p in range(chunk // 128):
                    total = total + value[:, p * 128 : (p + 1) * 128]
                col_sum[:, there] += jnp.sum(value.reshape(chunk // 8, 8, chunk), axis=0)
            row_sum[here, :] = total
            return carry

        lax.fori_loop(first_row, last_row, step, 0)

    norm_of(0, 1)
    gather.start(*[("z", s, 2, 0) for s in both], ("x", 1, "far"), ("y", -1, "far"))
    gather.start(*[(axis, s, "side", t) for t in both for axis in "yx" for s in both])
    gather.start(*[("z", s, 2, 1) for s in both], ("x", -1, "far"), ("y", 1, "far"), ("c", 1), ("c", -1))
    gather.wait(*[(axis, s, "own", g) for axis in "xy" for s in both for g in (0, 1)])
    norm_of(1, 5)
    gather.wait(("c", 0), ("c", 1), ("c", -1))
    work(0, 3, 0, 2)
    gather.start(*[("z", s, 3, 0) for s in both])
    gather.start(*[(axis, s, "across") for axis in "yx" for s in both])
    gather.start(*[(axis, s, "side far", t) for t in both for axis in "yx" for s in both])
    gather.start(*[("z", s, 3, 1) for s in both], ("c", 2), ("c", -2))
    gather.wait(*[(axis, s, "far") for axis in "xy" for s in both])
    norm_of(5, 11)
    work(0, 3, 2, 5)
    gather.start(("z", 1, 4, 0), ("z", -1, 4, 1))
    gather.start(*[(axis, s, "across far") for axis in "yx" for s in both])
    gather.wait(("c", 2), ("c", -2))
    work(3, 5, 0, 5)
    gather.start(("c", 3), ("c", -3), ("c", 4))
    gather.wait(*[(axis, s, "side far", t) for t in both for axis in "yx" for s in both])
    norm_of(11, 15)
    work(0, 5, 5, 7)
    gather.wait(("c", 3), ("c", -3))
    work(5, 7, 0, 7)
    gather.wait(*gather.made)
    norm_of(15, 16)
    work(0, 7, 7, 8)
    work(7, 8, 0, 8)

    def row_total(i, carry):
        place = (z + (i + 1) // 2 * (2 * (i % 2) - 1) + Z) % Z
        row_mass[pl.ds(place, 1), :] = to_row(jnp.sum(row_sum[span(i * chunk, chunk), :], axis=1, keepdims=True))
        return carry

    lax.fori_loop(0, Z, row_total, 0)

    def absolute(slot):
        dx, dy = AROUND[slot]
        return span(((y + dy + Y) % Y * X + (x + dx + X) % X) * rows, rows)

    column_total = jnp.sum(col_sum[...], axis=0, keepdims=True)
    for i in range(PLANE):
        col_mass[0:1, absolute(i)] = column_total[:, i * rows : (i + 1) * rows]

    mass = Gather(m_send, m_recv)
    mass.add("c", lambda mine_, send, recv: copy(row_mass, row_in, send, recv, sibling))

    def direct(source, target, mate, size, at, d):
        def make(sender, send, recv):
            return copy(source, target.at[at if sender else (at - d + size) % size], send, recv, mate(d))

        return make

    for d in range(1, X):
        mass.add(("x", d), direct(col_mass, col_ins, x_mate, X, x, d))
    for d in range(1, Y):
        mass.add(("y", d), direct(col_part, col_ins2, y_mate, Y, y, d))
    for d in range(1, Z):
        mass.add(("z", d), direct(row_pair, row_ins, z_mate, Z, z, d))
    mass.start("c", *[("x", d) for d in range(1, X)])
    col_ins[x] = col_mass[...]
    mass.wait("c")
    row_pair[...] = row_mass[...] + row_in[...]
    mass.start(*[("z", d) for d in range(1, Z)])
    row_ins[z] = row_pair[...]
    mass.wait(*[("x", d) for d in range(1, X)])
    col_part[...] = jnp.sum(col_ins[...], axis=0)
    mass.start(*[("y", d) for d in range(1, Y)])
    col_ins2[y] = col_part[...]
    mass.wait(*mass.made)
    mass.finish()
    row_mass[...] = 1.0 / jnp.sum(row_ins[...], axis=0)
    col_mass[...] = 1.0 / jnp.sum(col_ins2[...], axis=0)
    for i in range(PLANE):
        col_part[0:1, i * rows : (i + 1) * rows] = col_mass[0:1, absolute(i)]

    def pair_copy(n):
        return copy(sib_out.at[n], sib_in.at[n], s_send.at[n], s_recv.at[n], sibling)

    def run_copy(s, m, q):
        here = pl.ds(q * quarter, quarter)
        at = (s * 4 + m) * 4 + q
        return copy(
            run_out.at[s * 4 + m, here], run_in.at[s * 4 + m, here], r_send.at[at], r_recv.at[at], z_mate(2 * s - 1)
        )

    def comes(s, m, q):
        return m > 0 or q // 2 == 1 - s

    def link(m):
        for s in (0, 1):
            pair_copy(2 * m + 1 + s).wait_recv()
        for q in range(4):
            here = slice(q * quarter, (q + 1) * quarter)
            for s in (1, 0):
                n = 2 * m + 1 + s
                total = mine[n, here, :] + sib_in[n, here, :].astype(SINGLE)
                if comes(s, m, q):
                    run_copy(s, m, q).wait_recv()
                    total = total + run_in[s * 4 + m, here, :].astype(SINGLE)
                run_out[s * 4 + m + 1, here, :] = total.astype(HALF)
                run_copy(s, m + 1, q).start()

    def pull_step(n, carry):
        j = Z - 1 - n
        i = (z + (j + 1) // 2 * (2 * (j % 2) - 1) + Z) % Z
        here = span(j * chunk, chunk)
        inverse = to_column(row_mass[pl.ds(i, 1), :])
        total = jnp.zeros((chunk, 1), SINGLE)
        moved = jnp.zeros((chunk, embed), SINGLE)
        width = 2 * chunk
        for j in range(PLANE * rows // width):
            there = slice(j * width, (j + 1) * width)
            pair = ((inverse + col_part[0:1, there]) * tile[here, there]).astype(HALF)
            total = total + jnp.sum(pair.astype(SINGLE), axis=1, keepdims=True)
            moved = moved + jnp.dot(pair, planes[there, :], preferred_element_type=SINGLE)
        pull = lines[here, :].astype(SINGLE) * total - moved
        mine[n] = jnp.where(k == 0, pull[0:rows, :], pull[rows:chunk, :])
        sib_out[n] = jnp.where(k == 0, pull[rows:chunk, :], pull[0:rows, :]).astype(HALF)
        pair_copy(n).start()

        @pl.when(n == 1)
        def _():
            pair_copy(0).wait_recv()
            far = (mine[0] + sib_in[0].astype(SINGLE)).astype(HALF)
            run_out[4] = far
            run_out[0] = far
            for q in range(4):
                run_copy(1 - q // 2, 0, q).start()

        for m, after in ((0, 3), (1, 6), (2, 7)):

            @pl.when(n == after)
            def _():
                link(m)

        return carry

    lax.fori_loop(0, Z, pull_step, 0)
    pair_copy(Z - 1).wait_recv()
    pull = mine[Z - 1] + sib_in[Z - 1].astype(SINGLE)
    for q in range(4):
        for s in (1, 0):
            run_copy(s, 3, q).wait_recv()
    for s in (1, 0):
        pull = pull + run_in[s * 4 + 3].astype(SINGLE)
    gradient = jnp.where(live > 0.5, 0.5 * pull, 0.0).astype(HALF)

    gradients[0:rows, :] = gradient
    terms = Gather(w_send, w_recv)
    terms.add("c", lambda mine_, send, recv: copy(gradients.at[span(0, rows)], gradients.at[span(rows, rows)], send, recv, sibling))
    terms.start("c")
    embed_out[...] = gradient
    stores = [pltpu.make_async_copy(embed_out, grad_embed, store.at[0])]
    stores[0].start()
    gather.wait("feats")
    split = embed // 2
    share = group // XH

    def first(table, axis, mate, size, at, d):
        def make(sender, send, recv):
            return copy(
                first_out.at[table, (at + d) % size],
                first_in.at[table, at if sender else (at - d + size) % size],
                send, recv, mate(d),
            )

        return make

    def second(table, mate, size, at, d):
        def make(sender, send, recv):
            return copy(
                second_out.at[table, (at + d) % size],
                second_in.at[table, at if sender else (at - d + size) % size],
                send, recv, mate(d),
            )

        return make

    def third(d):
        def make(sender, send, recv):
            return copy(third_out.at[(z + d) % Z], third_in.at[z if sender else (z - d + Z) % Z], send, recv, z_mate(d))

        return make

    for d in range(1, X):
        terms.add(("first", 0, d), first(0, "x", x_mate, X, x, d))
        terms.add(("second", 1, d), second(1, x_mate, X, x, d))
    for d in range(1, Y):
        terms.add(("first", 1, d), first(1, "y", y_mate, Y, y, d))
        terms.add(("second", 0, d), second(0, y_mate, Y, y, d))
    for d in range(1, Z):
        terms.add(("third", d), third(d))

    terms.wait("c")
    both_gradients = gradients[...]
    for g in range(Y * XL):
        to_y, low = g // XL, g % XL
        term = (tn(mixed[:, g * group : (g + 1) * group], both_gradients) * scale).astype(HALF)
        for high in range(XH):
            to_x = high * XL + low
            piece = term[high * share : (high + 1) * share, :]
            first_out[0, to_x, to_y * share : (to_y + 1) * share, :] = piece[:, 0:split]
            first_out[1, to_y, to_x * share : (to_x + 1) * share, :] = piece[:, split:embed]
    for d in range(1, X):
        terms.start(("first", 0, d), ("first", 1, d))
    feats_out[...] = nt(gradient, weight[...]).astype(HALF)
    stores.append(pltpu.make_async_copy(feats_out, grad_feats, store.at[1]))
    stores[1].start()
    for table, at in ((0, x), (1, y)):
        first_in[table, at] = first_out[table, at]
        terms.wait(*[("first", table, d) for d in range(1, X)])
        added = jnp.sum(first_in[table].astype(SINGLE), axis=0).astype(HALF)
        for i in range(4):
            second_out[table, i] = added[i * share : (i + 1) * share, :]
        terms.start(*[("second", table, d) for d in range(1, X)])
    for table, at in ((0, y), (1, x)):
        second_in[table, at] = second_out[table, at]
        terms.wait(*[("second", table, d) for d in range(1, X)])
        added = jnp.sum(second_in[table].astype(SINGLE), axis=0)
        for i in range(Z):
            third_out[i, :, table * split : (table + 1) * split] = added[i * (share // Z) : (i + 1) * (share // Z), :]
    terms.start(*[("third", d) for d in range(1, Z)])
    third_in[z] = third_out[z]
    terms.wait(*terms.made)
    weight_out[...] = jnp.sum(third_in[...], axis=0)
    stores.append(pltpu.make_async_copy(weight_out, grad_weight, store.at[2]))
    stores[2].start()

    gather.finish()
    terms.finish()
    for n in range(Z):
        pair_copy(n).wait_send()
    for s in (0, 1):
        for m in range(4):
            for q in range(4):
                if comes(s, m, q):
                    run_copy(s, m, q).wait_send()
    for one in stores:
        one.wait()


def place(*refs):
    sources, targets, held, get, put = refs[0:3], refs[3:6], refs[6:9], refs[9], refs[10]
    gets = [pltpu.make_async_copy(a, b, get.at[i]) for i, (a, b) in enumerate(zip(sources, held))]
    puts = [pltpu.make_async_copy(a, b, put.at[i]) for i, (a, b) in enumerate(zip(held, targets))]
    for one in gets:
        one.start()
    for one, other in zip(gets, puts):
        one.wait()
        other.start()
    for one in puts:
        one.wait()


def local(feats, weight, valid):
    rows, width = feats.shape
    embed = weight.shape[1]
    frames = rows * LINE * PLANE
    out_rows = width // (LINE * PLANE)
    hbm = pl.BlockSpec(memory_space=pl.ANY)

    def half(*shape):
        return pltpu.VMEM(shape, HALF)

    def single(*shape):
        return pltpu.VMEM(shape, SINGLE)

    def dma(n):
        return [pltpu.SemaphoreType.DMA((n,))] * 2

    share = Z * out_rows
    columns = PLANE * rows
    shapes = (
        jax.ShapeDtypeStruct((rows, embed), HALF),
        jax.ShapeDtypeStruct((rows, width), HALF),
        jax.ShapeDtypeStruct((out_rows, embed), SINGLE),
    )
    results = pl.pallas_call(
        functools.partial(kernel, band=float(embed // 4), scale=math.sqrt(width) / frames),
        out_shape=shapes,
        in_specs=[hbm] * 3,
        out_specs=(hbm,) * 3,
        scratch_shapes=[
            half(rows, width), half(width, embed), pltpu.VMEM((1, rows), jnp.int32),
            half(rows, embed), half(rows, width), single(out_rows, embed),
            half(LINE * rows, embed), half(columns, embed), single(1, columns), single(LINE * rows, columns),
            single(LINE * rows, 128), single(LINE * rows, 128), single(8, columns),
            single(Z, C * rows), single(Z, C * rows), single(Z, C * rows), single(Z, Z, C * rows),
            single(1, columns), single(X, 1, columns), single(1, columns), single(Y, 1, columns),
            single(Z, rows, embed), half(Z, rows, embed), half(Z, rows, embed),
            half(8, rows, embed), half(8, rows, embed),
            half(2 * rows, width // 2), half(rows, width // 2), half(2 * rows, embed),
            half(2, 4, 4 * share, embed // 2), half(2, 4, 4 * share, embed // 2),
            half(2, 4, share, embed // 2), half(2, 4, share, embed // 2),
            single(Z, out_rows, embed), single(Z, out_rows, embed),
        ]
        + [pltpu.SemaphoreType.DMA((6,)), pltpu.SemaphoreType.DMA((3,))]
        + dma(64) + dma(14) + dma(Z) + dma(32) + dma(20),
        compiler_params=pltpu.CompilerParams(
            collective_id=0, has_side_effects=True, vmem_limit_bytes=56 * 1024 * 1024
        ),
    )(feats, weight, valid.reshape(1, rows))
    return pl.pallas_call(
        place,
        out_shape=shapes,
        in_specs=[hbm] * 3,
        out_specs=(hbm,) * 3,
        scratch_shapes=[pltpu.VMEM(one.shape, one.dtype) for one in shapes] + dma(3),
    )(*results)


def solution(mesh):
    spec = P(("row", "col"), None)
    return jax.shard_map(
        local,
        mesh=mesh,
        in_specs=(spec, P(), P(("row", "col"))),
        out_specs=(spec, spec, spec),
        check_vma=False,
    )
```

```python
import functools
import math

import jax
import jax.numpy as jnp
from jax import lax
from jax.experimental import pallas as pl
from jax.experimental.pallas import tpu as pltpu
from jax.sharding import PartitionSpec as P

MESH = pl.DeviceIdType.MESH
XH, XL, Y, Z, C = 2, 2, 4, 8, 2
X = XH * XL
LINE = Z * C
PLANE = X * Y
FAR = 2.0**60
ALONG = (0, 1, -1, 2, -2, 3, -3, 4)
AROUND = (
    (0, 0), (1, 0), (-1, 0), (0, 1), (0, -1), (2, 0), (0, 2), (1, 1), (-1, 1), (1, -1), (-1, -1),
    (2, 1), (2, -1), (1, 2), (-1, 2), (2, 2),
)
HALF, SINGLE = jnp.bfloat16, jnp.float32


def line_slot(dz):
    return ALONG.index((dz + Z // 2 - 1) % Z - Z // 2 + 1)


def plane_slot(dx, dy):
    return AROUND.index(((dx + 1) % X - 1, (dy + 1) % Y - 1))


def device(x, y, z, k):
    return {"row": (y * XL + x % XL) * C + k, "col": (x // XL) * Z + z}


def to_row(column):
    n = column.shape[0]
    eye = lax.broadcasted_iota(jnp.int32, (n, n), 0) == lax.broadcasted_iota(jnp.int32, (n, n), 1)
    return jnp.sum(jnp.where(eye, column, 0.0), axis=0, keepdims=True)


def to_column(row):
    n = row.shape[1]
    eye = lax.broadcasted_iota(jnp.int32, (n, n), 0) == lax.broadcasted_iota(jnp.int32, (n, n), 1)
    return jnp.sum(jnp.where(eye, row, 0.0), axis=1, keepdims=True)


def nt(a, b):
    return lax.dot_general(a, b, (((1,), (1,)), ((), ())), preferred_element_type=SINGLE)


def tn(a, b):
    return lax.dot_general(a, b, (((0,), (0,)), ((), ())), preferred_element_type=SINGLE)


class Gather:
    def __init__(self, send, recv):
        self.send, self.recv = send, recv
        self.made, self.arrived = {}, set()

    def add(self, name, make, needs=()):
        number = len(self.made)
        self.made[name] = (lambda mine: make(mine, self.send.at[number], self.recv.at[number])), needs

    def start(self, *names):
        for name in names:
            make, needs = self.made[name]
            for need in needs:
                self.wait(need)
            make(True).start()

    def wait(self, *names):
        for name in names:
            if name not in self.arrived:
                self.arrived.add(name)
                self.made[name][0](False).wait_recv()

    def finish(self):
        for name in self.made:
            self.made[name][0](True).wait_send()


def kernel(
    feats_in, weight_in, valid_in,
    grad_embed, grad_feats, grad_weight,
    feats, weight, valid, embed_out, feats_out, weight_out,
    lines, planes, norms, tile, row_norm, row_sum, col_sum,
    row_mass, row_in, row_pair, row_ins, col_mass, col_ins, col_part, col_ins2,
    mine, sib_out, sib_in, run_out, run_in,
    mixed, leaving, turned, gradients, first_out, first_stop, first_in, second_out, second_in, third_out, third_in,
    load, store, g_send, g_recv, m_send, m_recv, s_send, s_recv, r_send, r_recv, w_send, w_recv,
    *, band, scale,
):
    rows, embed = grad_embed.shape
    r, c = lax.axis_index("row"), lax.axis_index("col")
    k, x, y, z = r % C, (c // Z) * XL + (r // C) % XL, r // (C * XL), c % Z
    sibling = device(x, y, z, 1 - k)

    def z_mate(d):
        return device(x, y, (z + d + Z) % Z, k)

    def x_mate(d):
        return device((x + d + X) % X, y, z, k)

    def y_mate(d):
        return device(x, (y + d + Y) % Y, z, k)

    barrier = pltpu.get_barrier_semaphore()
    friends = [sibling] + [z_mate(d) for d in range(1, Z)]
    friends += [x_mate(d) for d in range(1, X)] + [y_mate(d) for d in range(1, Y)]
    for friend in friends:
        pl.semaphore_signal(barrier, inc=1, device_id=friend, device_id_type=MESH)

    depth = weight.shape[0] // 4
    loads = [
        pltpu.make_async_copy(valid_in, valid, load.at[0]),
        pltpu.make_async_copy(feats_in, feats, load.at[1]),
    ]
    for i in range(4):
        part = pl.ds(i * depth, depth)
        loads.append(pltpu.make_async_copy(weight_in.at[part], weight.at[part], load.at[2 + i]))
    for one in loads:
        one.start()
    loads[0].wait()
    loads[1].wait()

    def span(start, n):
        return pl.ds(pl.multiple_of(start, n), n)

    def copy(src, dst, send, recv, target):
        return pltpu.make_async_remote_copy(
            src_ref=src, dst_ref=dst, send_sem=send, recv_sem=recv, device_id=target, device_id_type=MESH
        )

    live = to_column(jnp.where(valid[...] > 0, 1.0, 0.0))
    embedding = jnp.zeros((rows, embed), SINGLE)
    for i in range(4):
        loads[2 + i].wait()
        part = slice(i * depth, (i + 1) * depth)
        embedding = embedding + jnp.dot(feats[:, part], weight[part, :], preferred_element_type=SINGLE)
    away = jnp.where(lax.broadcasted_iota(jnp.int32, (rows, embed), 1) == 0, FAR, 0.0)
    own = jnp.where(live > 0.5, embedding, away).astype(HALF)
    lines[span(k * rows, rows), :] = own
    planes[0:rows, :] = own
    pl.semaphore_wait(barrier, len(friends))

    half, quarter = rows // 2, rows // 4
    gather = Gather(g_send, g_recv)

    def line_at(dz, core, start, n):
        return lines.at[span((line_slot(dz) * C + core) * rows + start, n)]

    def plane_at(dx, dy, start, n):
        return planes.at[pl.ds(plane_slot(dx, dy) * rows + start, n)]

    def along_z(s, d, q):
        at = (q if s == 1 else 3 - q) * quarter

        def make(sender, send, recv):
            source = line_at(-s * (d - 1), k, at, quarter)
            return copy(source, line_at(-s * d, k, at, quarter), send, recv, z_mate(s))

        return make

    for s in (1, -1):
        for d in range(1, Z // 2 + 1):
            for q in range(4 if d < Z // 2 else 2):
                gather.add(("z", s, d, q), along_z(s, d, q), [("z", s, d - 1, q)] if d > 1 else [])

    def across(o):
        def make(sender, send, recv):
            ref = line_at(o, k if sender else 1 - k, 0, rows)
            return copy(ref, ref, send, recv, sibling)

        return make

    for o in range(-Z // 2 + 1, Z // 2 + 1):
        if o == 0:
            needs = []
        elif o == Z // 2:
            needs = [("z", s, o, q) for s in (1, -1) for q in (0, 1)]
        else:
            needs = [("z", -1 if o > 0 else 1, abs(o), q) for q in range(4)]
        gather.add(("c", o), across(o), needs)

    def in_plane(axis, s, along, beside, start, n):
        def make(sender, send, recv):
            if axis == "x":
                source, target = plane_at(along, beside, start, n), plane_at(along - s, beside, start, n)
                return copy(source, target, send, recv, x_mate(s))
            source, target = plane_at(beside, along, start, n), plane_at(beside, along - s, start, n)
            return copy(source, target, send, recv, y_mate(s))

        return make

    for axis, other, h in (("y", "x", 0), ("x", "y", 1)):
        for s in (1, -1):
            part = 0 if s == 1 else 1
            for g in (0, 1):
                gather.add((axis, s, "own", g), in_plane(axis, s, 0, 0, g * half, half))
            gather.add((axis, s, "far"), in_plane(axis, s, -s, 0, part * half, half), [(axis, s, "own", part)])
            for t in (1, -1):
                gather.add((axis, s, "side", t), in_plane(axis, s, 0, t, h * half, half), [(other, -t, "own", h)])
                gather.add(
                    (axis, s, "side far", t),
                    in_plane(axis, s, -s, t, h * half + part * quarter, quarter),
                    [(axis, s, "side", t)],
                )
            gather.add(
                (axis, s, "across"),
                in_plane(axis, s, 0, 2, h * half, half),
                [(other, 1 if h == 0 else -1, "far")],
            )
            gather.add(
                (axis, s, "across far"),
                in_plane(axis, s, -s, 2, h * half + part * quarter, quarter),
                [(axis, s, "across")],
            )

    def swap_copy(mine_, send, recv):
        return copy(leaving, mixed.at[span(rows, rows)], send, recv, sibling)

    gather.add("feats", swap_copy)

    both = (1, -1)
    def pass_z(d, *pieces):
        gather.start(*[("z", s, d, q) for q in pieces for s in both])

    gather.start(*[("x", s, "own", 0) for s in both], *[("y", s, "own", 1) for s in both])
    pass_z(1, 0, 1)
    gather.start(*[("x", s, "own", 1) for s in both], *[("y", s, "own", 0) for s in both])
    pass_z(1, 2, 3)
    gather.start(("c", 0))

    group = XH * Z * grad_weight.shape[0]
    for g in range(Y * XL):
        low, high = feats[:, 2 * g * group : (2 * g + 1) * group], feats[:, (2 * g + 1) * group : (2 * g + 2) * group]
        here = slice(g * group, (g + 1) * group)
        mixed[0:rows, here] = jnp.where(k == 0, low, high)
        leaving[:, here] = jnp.where(k == 0, high, low)
    gather.start("feats")

    def norm_of(first, last):
        for i in range(first, last):
            here = slice(i * rows, (i + 1) * rows)
            wide = planes[here, :].astype(SINGLE)
            norms[0:1, here] = to_row(jnp.sum(wide * wide, axis=1, keepdims=True))

    chunk = C * rows
    rate = -1.0 / (band * math.log(2.0))

    def work(first_row, last_row, first_unit, last_unit):
        def step(i, carry):
            here = span(i * chunk, chunk)
            block = lines[here, :]
            if first_unit == 0:
                wide = block.astype(SINGLE)
                norm = jnp.broadcast_to(jnp.sum(wide * wide, axis=1, keepdims=True), (chunk, 128))
                row_norm[here, :] = norm
                total = jnp.zeros((chunk, 128), SINGLE)
            else:
                norm = row_norm[here, :]
                total = row_sum[here, :]
            norm = jnp.concatenate([norm] * (chunk // 128), axis=1)
            twice = block * 2
            for j in range(first_unit, last_unit):
                there = slice(j * chunk, (j + 1) * chunk)
                distance = (norm + norms[0:1, there]) - nt(twice, planes[there, :])
                value = jnp.exp2(distance * rate)
                tile[here, there] = value
                for p in range(chunk // 128):
                    total = total + value[:, p * 128 : (p + 1) * 128]
                col_sum[:, there] += jnp.sum(value.reshape(chunk // 8, 8, chunk), axis=0)
            row_sum[here, :] = total
            return carry

        lax.fori_loop(first_row, last_row, step, 0)

    col_sum[...] = jnp.zeros_like(col_sum)
    norm_of(0, 1)
    pass_z(2, 0)
    gather.start(("x", 1, "far"), ("y", -1, "far"))
    gather.start(*[(axis, s, "side", t) for t in both for axis in "yx" for s in both])
    pass_z(2, 1, 2, 3)
    gather.start(("x", -1, "far"), ("y", 1, "far"), ("c", 1), ("c", -1))
    gather.wait(*[(axis, s, "own", g) for axis in "xy" for s in both for g in (0, 1)])
    norm_of(1, 5)
    pass_z(3, 0, 1)
    gather.wait(("c", 0), ("c", 1), ("c", -1))
    work(0, 3, 0, 2)
    pass_z(3, 2, 3)
    gather.start(("c", 2), ("c", -2))
    gather.start(*[(axis, s, "across") for axis in "yx" for s in both])
    pass_z(4, 0, 1)
    gather.start(*[(axis, s, "side far", t) for t in both for axis in "yx" for s in both])
    gather.wait(*[(axis, s, "far") for axis in "xy" for s in both])
    norm_of(5, 11)
    work(0, 3, 2, 5)
    gather.start(*[(axis, s, "across far") for axis in "yx" for s in both])
    gather.start(("c", 3), ("c", -3), ("c", 4))
    gather.wait(("c", 2), ("c", -2))
    work(3, 5, 0, 5)
    gather.wait(*[(axis, s, "side far", t) for t in both for axis in "yx" for s in both])
    norm_of(11, 15)
    work(0, 5, 5, 7)
    gather.wait(("c", 3), ("c", -3))
    work(5, 7, 0, 7)
    gather.wait(*[(axis, s, "across far") for axis in "xy" for s in both])
    norm_of(15, 16)
    work(0, 7, 7, 8)
    gather.wait(*gather.made)
    work(7, 8, 0, 8)

    def absolute(slot):
        dx, dy = AROUND[slot]
        return span(((y + dy + Y) % Y * X + (x + dx + X) % X) * rows, rows)

    column_total = jnp.sum(col_sum[...], axis=0, keepdims=True)
    for i in range(PLANE):
        col_mass[0:1, absolute(i)] = column_total[:, i * rows : (i + 1) * rows]

    mass = Gather(m_send, m_recv)
    mass.add("c", lambda mine_, send, recv: copy(row_mass, row_in, send, recv, sibling))

    def direct(source, target, mate, size, at, d):
        def make(sender, send, recv):
            return copy(source, target.at[at if sender else (at - d + size) % size], send, recv, mate(d))

        return make

    for d in range(1, X):
        mass.add(("x", d), direct(col_mass, col_ins, x_mate, X, x, d))
    for d in range(1, Y):
        mass.add(("y", d), direct(col_part, col_ins2, y_mate, Y, y, d))
    for d in range(1, Z):
        mass.add(("z", d), direct(row_pair, row_ins, z_mate, Z, z, d))
    mass.start(*[("x", d) for d in range(1, X)])
    col_ins[x] = col_mass[...]

    def row_total(i, carry):
        place = (z + (i + 1) // 2 * (2 * (i % 2) - 1) + Z) % Z
        row_mass[pl.ds(place, 1), :] = to_row(jnp.sum(row_sum[span(i * chunk, chunk), :], axis=1, keepdims=True))
        return carry

    lax.fori_loop(0, Z, row_total, 0)
    mass.start("c")
    mass.wait("c")
    row_pair[...] = row_mass[...] + row_in[...]
    mass.start(*[("z", d) for d in range(1, Z)])
    row_ins[z] = row_pair[...]
    mass.wait(*[("x", d) for d in range(1, X)])
    col_part[...] = jnp.sum(col_ins[...], axis=0)
    mass.start(*[("y", d) for d in range(1, Y)])
    col_ins2[y] = col_part[...]
    for g in range(Y * XL):
        here = slice(g * group, (g + 1) * group)
        turned[here, :] = mixed[:, here].T
    mass.wait(*mass.made)
    mass.finish()
    row_mass[...] = 1.0 / jnp.sum(row_ins[...], axis=0)
    col_mass[...] = 1.0 / jnp.sum(col_ins2[...], axis=0)
    for i in range(PLANE):
        col_part[0:1, i * rows : (i + 1) * rows] = col_mass[0:1, absolute(i)]

    def pair_copy(n):
        return copy(sib_out.at[n], sib_in.at[n], s_send.at[n], s_recv.at[n], sibling)

    def run_copy(s, m, q):
        here = pl.ds(q * quarter, quarter)
        at = (s * 4 + m) * 4 + q
        return copy(
            run_out.at[s * 4 + m, here], run_in.at[s * 4 + m, here], r_send.at[at], r_recv.at[at], z_mate(2 * s - 1)
        )

    def comes(s, m, q):
        return m > 0 or q // 2 == 1 - s

    def link(m):
        for s in (0, 1):
            pair_copy(2 * m + 1 + s).wait_recv()
        for q in range(4):
            here = slice(q * quarter, (q + 1) * quarter)
            for s in (1, 0):
                n = 2 * m + 1 + s
                total = mine[n, here, :] + sib_in[n, here, :].astype(SINGLE)
                if comes(s, m, q):
                    run_copy(s, m, q).wait_recv()
                    total = total + run_in[s * 4 + m, here, :].astype(SINGLE)
                run_out[s * 4 + m + 1, here, :] = total.astype(HALF)
                run_copy(s, m + 1, q).start()

    def pull_step(n, carry):
        j = Z - 1 - n
        i = (z + (j + 1) // 2 * (2 * (j % 2) - 1) + Z) % Z
        here = span(j * chunk, chunk)
        inverse = to_column(row_mass[pl.ds(i, 1), :])
        total = jnp.zeros((chunk, 1), SINGLE)
        moved = jnp.zeros((chunk, embed), SINGLE)
        width = 2 * chunk
        for j in range(PLANE * rows // width):
            there = slice(j * width, (j + 1) * width)
            pair = ((inverse + col_part[0:1, there]) * tile[here, there]).astype(HALF)
            total = total + jnp.sum(pair.astype(SINGLE), axis=1, keepdims=True)
            moved = moved + jnp.dot(pair, planes[there, :], preferred_element_type=SINGLE)
        pull = lines[here, :].astype(SINGLE) * total - moved
        mine[n] = jnp.where(k == 0, pull[0:rows, :], pull[rows:chunk, :])
        sib_out[n] = jnp.where(k == 0, pull[rows:chunk, :], pull[0:rows, :]).astype(HALF)
        pair_copy(n).start()

        @pl.when(n == 1)
        def _():
            pair_copy(0).wait_recv()
            far = (mine[0] + sib_in[0].astype(SINGLE)).astype(HALF)
            run_out[4] = far
            run_out[0] = far
            for q in range(4):
                run_copy(1 - q // 2, 0, q).start()

        for m, after in ((0, 3), (1, 6), (2, 7)):

            @pl.when(n == after)
            def _():
                link(m)

        return carry

    lax.fori_loop(0, Z, pull_step, 0)
    pair_copy(Z - 1).wait_recv()
    terms = Gather(w_send, w_recv)

    def swap_gradient(q):
        def make(sender, send, recv):
            source, target = gradients.at[pl.ds(q * quarter, quarter)], gradients.at[pl.ds(rows + q * quarter, quarter)]
            return copy(source, target, send, recv, sibling)

        return make

    for q in range(4):
        here = slice(q * quarter, (q + 1) * quarter)
        pull = mine[Z - 1, here, :] + sib_in[Z - 1, here, :].astype(SINGLE)
        for s in (1, 0):
            run_copy(s, 3, q).wait_recv()
            pull = pull + run_in[s * 4 + 3, here, :].astype(SINGLE)
        gradients[here, :] = jnp.where(live[here, :] > 0.5, 0.5 * pull, 0.0).astype(HALF)
        terms.add(("c", q), swap_gradient(q))
        terms.start(("c", q))
    gradient = gradients[0:rows, :]

    embed_out[...] = gradient
    stores = [pltpu.make_async_copy(embed_out, grad_embed, store.at[0])]
    stores[0].start()
    gather.wait("feats")
    split = embed // 2
    share = group // XH

    side = 2 * share

    def first_copy(table, s, step):
        mate, size, at = (x_mate, X, x) if table == 0 else (y_mate, Y, y)
        near, far = (at + s + size) % size, (at + 2) % size
        low = s == 1
        way = 0 if s == 1 else 1
        stepped, plain = pl.ds(0 if low else side, side), pl.ds(side if low else 0, side)

        def make(sender, send, recv):
            if step == 0:
                return copy(first_out.at[table, far, stepped], first_stop.at[table, way], send, recv, mate(s))
            rows_of = plain if step == 1 else stepped
            return copy(first_out.at[table, near, rows_of], first_in.at[table, way, rows_of], send, recv, mate(s))

        return make

    def second(table, mate, size, at, d):
        def make(sender, send, recv):
            return copy(
                second_out.at[table, (at + d) % size],
                second_in.at[table, at if sender else (at - d + size) % size],
                send, recv, mate(d),
            )

        return make

    def third(d):
        def make(sender, send, recv):
            return copy(third_out.at[(z + d) % Z], third_in.at[z if sender else (z - d + Z) % Z], send, recv, z_mate(d))

        return make

    for table in (0, 1):
        for s in both:
            for step in range(3):
                terms.add(("first", table, s, step), first_copy(table, s, step))
    for d in range(1, X):
        terms.add(("second", 1, d), second(1, x_mate, X, x, d))
    for d in range(1, Y):
        terms.add(("second", 0, d), second(0, y_mate, Y, y, d))
    for d in range(1, Z):
        terms.add(("third", d), third(d))

    terms.wait(*[("c", q) for q in range(4)])
    both_gradients = gradients[...]
    for g in range(Y * XL):
        to_y, low = g // XL, g % XL
        term = (
            jnp.dot(turned[g * group : (g + 1) * group, :], both_gradients, preferred_element_type=SINGLE) * scale
        ).astype(HALF)
        for high in range(XH):
            to_x = high * XL + low
            piece = term[high * share : (high + 1) * share, :]
            first_out[0, to_x, to_y * share : (to_y + 1) * share, :] = piece[:, 0:split]
            first_out[1, to_y, to_x * share : (to_x + 1) * share, :] = piece[:, split:embed]
    for step in (0, 1):
        terms.start(*[("first", table, s, step) for table in (0, 1) for s in both])
    feats_out[...] = nt(gradient, weight[...]).astype(HALF)
    gather.finish()
    for n in range(Z):
        pair_copy(n).wait_send()
    for s in (0, 1):
        for m in range(4):
            for q in range(4):
                if comes(s, m, q):
                    run_copy(s, m, q).wait_send()
    stores.append(pltpu.make_async_copy(feats_out, grad_feats, store.at[1]))
    stores[1].start()
    for table, at in ((0, x), (1, y)):
        for s in both:
            terms.wait(("first", table, s, 0))
            near, way = (at + s + 4) % 4, 0 if s == 1 else 1
            here = slice(0, side) if s == 1 else slice(side, 2 * side)
            passed = first_out[table, near, here].astype(SINGLE) + first_stop[table, way].astype(SINGLE)
            first_out[table, near, here] = passed.astype(HALF)
            terms.start(("first", table, s, 2))
    for table, at in ((0, x), (1, y)):
        terms.wait(*[("first", table, s, step) for s in both for step in (1, 2)])
        added = first_out[table, at].astype(SINGLE)
        added = (added + first_in[table, 0].astype(SINGLE) + first_in[table, 1].astype(SINGLE)).astype(HALF)
        for i in range(4):
            second_out[table, i] = added[i * share : (i + 1) * share, :]
        terms.start(*[("second", table, d) for d in range(1, X)])
    totals = []
    for table, at in ((0, y), (1, x)):
        second_in[table, at] = second_out[table, at]
        terms.wait(*[("second", table, d) for d in range(1, X)])
        totals.append(jnp.sum(second_in[table].astype(SINGLE), axis=0))
    few = share // Z
    for i in range(Z):
        here = slice(i * few, (i + 1) * few)
        third_out[i] = jnp.concatenate([total[here, :] for total in totals], axis=0).astype(HALF)
    terms.start(*[("third", d) for d in range(1, Z)])
    third_in[z] = third_out[z]
    terms.wait(*terms.made)
    summed = jnp.sum(third_in[...].astype(SINGLE), axis=0)
    weight_out[...] = jnp.concatenate([summed[0:few, :], summed[few : 2 * few, :]], axis=1)
    stores.append(pltpu.make_async_copy(weight_out, grad_weight, store.at[2]))
    stores[2].start()

    terms.finish()
    for one in stores:
        one.wait()


def place(*refs):
    sources, targets, held, get, put = refs[0:3], refs[3:6], refs[6:9], refs[9], refs[10]
    gets = [pltpu.make_async_copy(a, b, get.at[i]) for i, (a, b) in enumerate(zip(sources, held))]
    puts = [pltpu.make_async_copy(a, b, put.at[i]) for i, (a, b) in enumerate(zip(held, targets))]
    for one in gets:
        one.start()
    for one, other in zip(gets, puts):
        one.wait()
        other.start()
    for one in puts:
        one.wait()


def local(feats, weight, valid):
    rows, width = feats.shape
    embed = weight.shape[1]
    frames = rows * LINE * PLANE
    out_rows = width // (LINE * PLANE)
    hbm = pl.BlockSpec(memory_space=pl.ANY)

    def half(*shape):
        return pltpu.VMEM(shape, HALF)

    def single(*shape):
        return pltpu.VMEM(shape, SINGLE)

    def dma(n):
        return [pltpu.SemaphoreType.DMA((n,))] * 2

    share = Z * out_rows
    columns = PLANE * rows
    shapes = (
        jax.ShapeDtypeStruct((rows, embed), HALF),
        jax.ShapeDtypeStruct((rows, width), HALF),
        jax.ShapeDtypeStruct((out_rows, embed), SINGLE),
    )
    results = pl.pallas_call(
        functools.partial(kernel, band=float(embed // 4), scale=math.sqrt(width) / frames),
        out_shape=shapes,
        in_specs=[hbm] * 3,
        out_specs=(hbm,) * 3,
        scratch_shapes=[
            half(rows, width), half(width, embed), pltpu.VMEM((1, rows), jnp.int32),
            half(rows, embed), half(rows, width), single(out_rows, embed),
            half(LINE * rows, embed), half(columns, embed), single(1, columns), single(LINE * rows, columns),
            single(LINE * rows, 128), single(LINE * rows, 128), single(8, columns),
            single(Z, C * rows), single(Z, C * rows), single(Z, C * rows), single(Z, Z, C * rows),
            single(1, columns), single(X, 1, columns), single(1, columns), single(Y, 1, columns),
            single(Z, rows, embed), half(Z, rows, embed), half(Z, rows, embed),
            half(8, rows, embed), half(8, rows, embed),
            half(2 * rows, width // 2), half(rows, width // 2), half(width // 2, 2 * rows), half(2 * rows, embed),
            half(2, 4, 4 * share, embed // 2), half(2, 2, 2 * share, embed // 2), half(2, 2, 4 * share, embed // 2),
            half(2, 4, share, embed // 2), half(2, 4, share, embed // 2),
            half(Z, 2 * out_rows, embed // 2), half(Z, 2 * out_rows, embed // 2),
        ]
        + [pltpu.SemaphoreType.DMA((6,)), pltpu.SemaphoreType.DMA((3,))]
        + dma(80) + dma(14) + dma(Z) + dma(32) + dma(29),
        compiler_params=pltpu.CompilerParams(
            collective_id=0, has_side_effects=True, vmem_limit_bytes=56 * 1024 * 1024
        ),
    )(feats, weight, valid.reshape(1, rows))
    return pl.pallas_call(
        place,
        out_shape=shapes,
        in_specs=[hbm] * 3,
        out_specs=(hbm,) * 3,
        scratch_shapes=[pltpu.VMEM(one.shape, one.dtype) for one in shapes] + dma(3),
    )(*results)


def solution(mesh):
    spec = P(("row", "col"), None)
    return jax.shard_map(
        local,
        mesh=mesh,
        in_specs=(spec, P(), P(("row", "col"))),
        out_specs=(spec, spec, spec),
        check_vma=False,
    )
```

```python
import functools
import math

import jax
import jax.numpy as jnp
from jax import lax
from jax.experimental import pallas as pl
from jax.experimental.pallas import tpu as pltpu
from jax.sharding import PartitionSpec as P

MESH = pl.DeviceIdType.MESH
XH, XL, Y, Z, C = 2, 2, 4, 8, 2
X = XH * XL
LINE = Z * C
PLANE = X * Y
FAR = 2.0**60
ALONG = (0, 1, -1, 2, -2, 3, -3, 4)
AROUND = (
    (0, 0), (1, 0), (-1, 0), (0, 1), (0, -1), (2, 0), (0, 2), (1, 1), (-1, 1), (1, -1), (-1, -1),
    (2, 1), (2, -1), (1, 2), (-1, 2), (2, 2),
)
HALF, SINGLE = jnp.bfloat16, jnp.float32


def line_slot(dz):
    return ALONG.index((dz + Z // 2 - 1) % Z - Z // 2 + 1)


def plane_slot(dx, dy):
    return AROUND.index(((dx + 1) % X - 1, (dy + 1) % Y - 1))


def device(x, y, z, k):
    return {"row": (y * XL + x % XL) * C + k, "col": (x // XL) * Z + z}


def to_row(column):
    n = column.shape[0]
    eye = lax.broadcasted_iota(jnp.int32, (n, n), 0) == lax.broadcasted_iota(jnp.int32, (n, n), 1)
    return jnp.sum(jnp.where(eye, column, 0.0), axis=0, keepdims=True)


def to_column(row):
    n = row.shape[1]
    eye = lax.broadcasted_iota(jnp.int32, (n, n), 0) == lax.broadcasted_iota(jnp.int32, (n, n), 1)
    return jnp.sum(jnp.where(eye, row, 0.0), axis=1, keepdims=True)


def nt(a, b):
    return lax.dot_general(a, b, (((1,), (1,)), ((), ())), preferred_element_type=SINGLE)


def tn(a, b):
    return lax.dot_general(a, b, (((0,), (0,)), ((), ())), preferred_element_type=SINGLE)


class Gather:
    def __init__(self, send, recv):
        self.send, self.recv = send, recv
        self.made, self.arrived = {}, set()

    def add(self, name, make, needs=()):
        number = len(self.made)
        self.made[name] = (lambda mine: make(mine, self.send.at[number], self.recv.at[number])), needs

    def start(self, *names):
        for name in names:
            make, needs = self.made[name]
            for need in needs:
                self.wait(need)
            make(True).start()

    def wait(self, *names):
        for name in names:
            if name not in self.arrived:
                self.arrived.add(name)
                self.made[name][0](False).wait_recv()

    def finish(self):
        for name in self.made:
            self.made[name][0](True).wait_send()


def kernel(
    feats_in, weight_in, valid_in,
    grad_embed, grad_feats, grad_weight,
    feats, weight, valid, embed_out, feats_out, weight_out,
    lines, planes, planes_t, norms, tile, row_norm, row_sum, col_sum,
    row_mass, row_in, row_pair, row_ins, col_mass, col_ins, col_part, col_ins2,
    mine, sib_out, sib_in, run_out, run_in,
    mixed, leaving, turned, gradients, first_out, first_stop, first_in, second_out, second_in, third_out, third_in,
    load, store, g_send, g_recv, m_send, m_recv, s_send, s_recv, r_send, r_recv, w_send, w_recv,
    *, band, scale,
):
    rows, embed = grad_embed.shape
    r, c = lax.axis_index("row"), lax.axis_index("col")
    k, x, y, z = r % C, (c // Z) * XL + (r // C) % XL, r // (C * XL), c % Z
    sibling = device(x, y, z, 1 - k)

    def z_mate(d):
        return device(x, y, (z + d + Z) % Z, k)

    def x_mate(d):
        return device((x + d + X) % X, y, z, k)

    def y_mate(d):
        return device(x, (y + d + Y) % Y, z, k)

    barrier = pltpu.get_barrier_semaphore()
    friends = [sibling] + [z_mate(d) for d in range(1, Z)]
    friends += [x_mate(d) for d in range(1, X)] + [y_mate(d) for d in range(1, Y)]
    for friend in friends:
        pl.semaphore_signal(barrier, inc=1, device_id=friend, device_id_type=MESH)

    depth = weight.shape[0] // 4
    loads = [
        pltpu.make_async_copy(valid_in, valid, load.at[0]),
        pltpu.make_async_copy(feats_in, feats, load.at[1]),
    ]
    for i in range(4):
        part = pl.ds(i * depth, depth)
        loads.append(pltpu.make_async_copy(weight_in.at[part], weight.at[part], load.at[2 + i]))
    for one in loads:
        one.start()
    loads[0].wait()
    loads[1].wait()

    def span(start, n):
        return pl.ds(pl.multiple_of(start, n), n)

    def copy(src, dst, send, recv, target):
        return pltpu.make_async_remote_copy(
            src_ref=src, dst_ref=dst, send_sem=send, recv_sem=recv, device_id=target, device_id_type=MESH
        )

    live = to_column(jnp.where(valid[...] > 0, 1.0, 0.0))
    embedding = jnp.zeros((rows, embed), SINGLE)
    for i in range(4):
        loads[2 + i].wait()
        part = slice(i * depth, (i + 1) * depth)
        embedding = embedding + jnp.dot(feats[:, part], weight[part, :], preferred_element_type=SINGLE)
    away = jnp.where(lax.broadcasted_iota(jnp.int32, (rows, embed), 1) == 0, FAR, 0.0)
    own = jnp.where(live > 0.5, embedding, away).astype(HALF)
    lines[span(k * rows, rows), :] = own
    planes[0:rows, :] = own
    pl.semaphore_wait(barrier, len(friends))

    half, quarter = rows // 2, rows // 4
    gather = Gather(g_send, g_recv)

    def line_at(dz, core, start, n):
        return lines.at[span((line_slot(dz) * C + core) * rows + start, n)]

    def plane_at(dx, dy, start, n):
        return planes.at[pl.ds(plane_slot(dx, dy) * rows + start, n)]

    def along_z(s, d, q):
        at = (q if s == 1 else 3 - q) * quarter

        def make(sender, send, recv):
            source = line_at(-s * (d - 1), k, at, quarter)
            return copy(source, line_at(-s * d, k, at, quarter), send, recv, z_mate(s))

        return make

    for s in (1, -1):
        for d in range(1, Z // 2 + 1):
            for q in range(4 if d < Z // 2 else 2):
                gather.add(("z", s, d, q), along_z(s, d, q), [("z", s, d - 1, q)] if d > 1 else [])

    def across(o):
        def make(sender, send, recv):
            ref = line_at(o, k if sender else 1 - k, 0, rows)
            return copy(ref, ref, send, recv, sibling)

        return make

    for o in range(-Z // 2 + 1, Z // 2 + 1):
        if o == 0:
            needs = []
        elif o == Z // 2:
            needs = [("z", s, o, q) for s in (1, -1) for q in (0, 1)]
        else:
            needs = [("z", -1 if o > 0 else 1, abs(o), q) for q in range(4)]
        gather.add(("c", o), across(o), needs)

    def in_plane(axis, s, along, beside, start, n):
        def make(sender, send, recv):
            if axis == "x":
                source, target = plane_at(along, beside, start, n), plane_at(along - s, beside, start, n)
                return copy(source, target, send, recv, x_mate(s))
            source, target = plane_at(beside, along, start, n), plane_at(beside, along - s, start, n)
            return copy(source, target, send, recv, y_mate(s))

        return make

    for axis, other, h in (("y", "x", 0), ("x", "y", 1)):
        for s in (1, -1):
            part = 0 if s == 1 else 1
            for g in (0, 1):
                gather.add((axis, s, "own", g), in_plane(axis, s, 0, 0, g * half, half))
            gather.add((axis, s, "far"), in_plane(axis, s, -s, 0, part * half, half), [(axis, s, "own", part)])
            for t in (1, -1):
                gather.add((axis, s, "side", t), in_plane(axis, s, 0, t, h * half, half), [(other, -t, "own", h)])
                gather.add(
                    (axis, s, "side far", t),
                    in_plane(axis, s, -s, t, h * half + part * quarter, quarter),
                    [(axis, s, "side", t)],
                )
            gather.add(
                (axis, s, "across"),
                in_plane(axis, s, 0, 2, h * half, half),
                [(other, 1 if h == 0 else -1, "far")],
            )
            gather.add(
                (axis, s, "across far"),
                in_plane(axis, s, -s, 2, h * half + part * quarter, quarter),
                [(axis, s, "across")],
            )

    def swap_copy(mine_, send, recv):
        return copy(leaving, mixed.at[span(rows, rows)], send, recv, sibling)

    gather.add("feats", swap_copy)

    both = (1, -1)
    def pass_z(d, *pieces):
        gather.start(*[("z", s, d, q) for q in pieces for s in both])

    gather.start(*[("x", s, "own", 0) for s in both], *[("y", s, "own", 1) for s in both])
    pass_z(1, 0, 1)
    gather.start(*[("x", s, "own", 1) for s in both], *[("y", s, "own", 0) for s in both])
    pass_z(1, 2, 3)
    gather.start(("c", 0))

    group = XH * Z * grad_weight.shape[0]
    for g in range(Y * XL):
        low, high = feats[:, 2 * g * group : (2 * g + 1) * group], feats[:, (2 * g + 1) * group : (2 * g + 2) * group]
        here = slice(g * group, (g + 1) * group)
        mixed[0:rows, here] = jnp.where(k == 0, low, high)
        leaving[:, here] = jnp.where(k == 0, high, low)
    gather.start("feats")

    def norm_of(first, last):
        for i in range(first, last):
            here = slice(i * rows, (i + 1) * rows)
            planes_t[:, here] = planes[here, :].T
            wide = planes[here, :].astype(SINGLE)
            norms[0:1, here] = to_row(jnp.sum(wide * wide, axis=1, keepdims=True))

    chunk = C * rows
    rate = -1.0 / (band * math.log(2.0))

    def work(first_row, last_row, first_unit, last_unit):
        def step(i, carry):
            here = span(i * chunk, chunk)
            block = lines[here, :]
            if first_unit == 0:
                wide = block.astype(SINGLE)
                norm = jnp.broadcast_to(jnp.sum(wide * wide, axis=1, keepdims=True), (chunk, 128))
                row_norm[here, :] = norm
                total = jnp.zeros((chunk, 128), SINGLE)
            else:
                norm = row_norm[here, :]
                total = row_sum[here, :]
            norm = jnp.concatenate([norm] * (chunk // 128), axis=1)
            twice = block * 2
            for j in range(first_unit, last_unit):
                there = slice(j * chunk, (j + 1) * chunk)
                distance = (norm + norms[0:1, there]) - jnp.dot(
                    twice, planes_t[:, there], preferred_element_type=SINGLE
                )
                value = jnp.exp2(distance * rate)
                tile[here, there] = value
                for p in range(chunk // 128):
                    total = total + value[:, p * 128 : (p + 1) * 128]
                col_sum[:, there] += jnp.sum(value.reshape(chunk // 8, 8, chunk), axis=0)
            row_sum[here, :] = total
            return carry

        lax.fori_loop(first_row, last_row, step, 0)

    col_sum[...] = jnp.zeros_like(col_sum)
    norm_of(0, 1)
    pass_z(2, 0)
    gather.start(("x", 1, "far"), ("y", -1, "far"))
    gather.start(*[(axis, s, "side", t) for t in both for axis in "yx" for s in both])
    pass_z(2, 1, 2, 3)
    gather.start(("x", -1, "far"), ("y", 1, "far"), ("c", 1), ("c", -1))
    gather.wait(*[(axis, s, "own", g) for axis in "xy" for s in both for g in (0, 1)])
    norm_of(1, 5)
    pass_z(3, 0, 1)
    gather.wait(("c", 0), ("c", 1), ("c", -1))
    work(0, 3, 0, 2)
    pass_z(3, 2, 3)
    gather.start(("c", 2), ("c", -2))
    gather.start(*[(axis, s, "across") for axis in "yx" for s in both])
    pass_z(4, 0, 1)
    gather.start(*[(axis, s, "side far", t) for t in both for axis in "yx" for s in both])
    gather.wait(*[(axis, s, "far") for axis in "xy" for s in both])
    norm_of(5, 11)
    work(0, 3, 2, 5)
    gather.start(*[(axis, s, "across far") for axis in "yx" for s in both])
    gather.start(("c", 3), ("c", -3), ("c", 4))
    gather.wait(("c", 2), ("c", -2))
    work(3, 5, 0, 5)
    gather.wait(*[(axis, s, "side far", t) for t in both for axis in "yx" for s in both])
    norm_of(11, 15)
    work(0, 5, 5, 7)
    gather.wait(("c", 3), ("c", -3))
    work(5, 7, 0, 7)
    gather.wait(*[(axis, s, "across far") for axis in "xy" for s in both])
    norm_of(15, 16)
    work(0, 7, 7, 8)
    gather.wait(*gather.made)
    work(7, 8, 0, 8)

    def absolute(slot):
        dx, dy = AROUND[slot]
        return span(((y + dy + Y) % Y * X + (x + dx + X) % X) * rows, rows)

    column_total = jnp.sum(col_sum[...], axis=0, keepdims=True)
    for i in range(PLANE):
        col_mass[0:1, absolute(i)] = column_total[:, i * rows : (i + 1) * rows]

    mass = Gather(m_send, m_recv)
    mass.add("c", lambda mine_, send, recv: copy(row_mass, row_in, send, recv, sibling))

    def direct(source, target, mate, size, at, d):
        def make(sender, send, recv):
            return copy(source, target.at[at if sender else (at - d + size) % size], send, recv, mate(d))

        return make

    for d in range(1, X):
        mass.add(("x", d), direct(col_mass, col_ins, x_mate, X, x, d))
    for d in range(1, Y):
        mass.add(("y", d), direct(col_part, col_ins2, y_mate, Y, y, d))
    for d in range(1, Z):
        mass.add(("z", d), direct(row_pair, row_ins, z_mate, Z, z, d))
    mass.start(*[("x", d) for d in range(1, X)])
    col_ins[x] = col_mass[...]

    def row_total(i, carry):
        place = (z + (i + 1) // 2 * (2 * (i % 2) - 1) + Z) % Z
        row_mass[pl.ds(place, 1), :] = to_row(jnp.sum(row_sum[span(i * chunk, chunk), :], axis=1, keepdims=True))
        return carry

    lax.fori_loop(0, Z, row_total, 0)
    mass.start("c")
    for g in range(Y * XL):
        here = slice(g * group, (g + 1) * group)
        turned[here, :] = mixed[:, here].T
    mass.wait("c")
    row_pair[...] = row_mass[...] + row_in[...]
    mass.start(*[("z", d) for d in range(1, Z)])
    row_ins[z] = row_pair[...]
    mass.wait(*[("x", d) for d in range(1, X)])
    col_part[...] = jnp.sum(col_ins[...], axis=0)
    mass.start(*[("y", d) for d in range(1, Y)])
    col_ins2[y] = col_part[...]
    mass.wait(*mass.made)
    mass.finish()
    row_mass[...] = 1.0 / jnp.sum(row_ins[...], axis=0)
    col_mass[...] = 1.0 / jnp.sum(col_ins2[...], axis=0)
    for i in range(PLANE):
        col_part[0:1, i * rows : (i + 1) * rows] = col_mass[0:1, absolute(i)]

    def pair_copy(n):
        return copy(sib_out.at[n], sib_in.at[n], s_send.at[n], s_recv.at[n], sibling)

    def run_copy(s, m, q):
        here = pl.ds(q * quarter, quarter)
        at = (s * 4 + m) * 4 + q
        return copy(
            run_out.at[s * 4 + m, here], run_in.at[s * 4 + m, here], r_send.at[at], r_recv.at[at], z_mate(2 * s - 1)
        )

    def comes(s, m, q):
        return m > 0 or q // 2 == 1 - s

    def link(m):
        for s in (0, 1):
            pair_copy(2 * m + 1 + s).wait_recv()
        for q in range(4):
            here = slice(q * quarter, (q + 1) * quarter)
            for s in (1, 0):
                n = 2 * m + 1 + s
                total = mine[n, here, :] + sib_in[n, here, :].astype(SINGLE)
                if comes(s, m, q):
                    run_copy(s, m, q).wait_recv()
                    total = total + run_in[s * 4 + m, here, :].astype(SINGLE)
                run_out[s * 4 + m + 1, here, :] = total.astype(HALF)
                run_copy(s, m + 1, q).start()

    def pull_step(n, carry):
        j = Z - 1 - n
        i = (z + (j + 1) // 2 * (2 * (j % 2) - 1) + Z) % Z
        here = span(j * chunk, chunk)
        inverse = to_column(row_mass[pl.ds(i, 1), :])
        total = jnp.zeros((chunk, 1), SINGLE)
        moved = jnp.zeros((chunk, embed), SINGLE)
        width = 2 * chunk
        for j in range(PLANE * rows // width):
            there = slice(j * width, (j + 1) * width)
            pair = ((inverse + col_part[0:1, there]) * tile[here, there]).astype(HALF)
            total = total + jnp.sum(pair.astype(SINGLE), axis=1, keepdims=True)
            moved = moved + jnp.dot(pair, planes[there, :], preferred_element_type=SINGLE)
        pull = lines[here, :].astype(SINGLE) * total - moved
        mine[n] = jnp.where(k == 0, pull[0:rows, :], pull[rows:chunk, :])
        sib_out[n] = jnp.where(k == 0, pull[rows:chunk, :], pull[0:rows, :]).astype(HALF)
        pair_copy(n).start()

        @pl.when(n == 1)
        def _():
            pair_copy(0).wait_recv()
            far = (mine[0] + sib_in[0].astype(SINGLE)).astype(HALF)
            run_out[4] = far
            run_out[0] = far
            for q in range(4):
                run_copy(1 - q // 2, 0, q).start()

        for m, after in ((0, 3), (1, 6), (2, 7)):

            @pl.when(n == after)
            def _():
                link(m)

        return carry

    lax.fori_loop(0, Z, pull_step, 0)
    pair_copy(Z - 1).wait_recv()
    terms = Gather(w_send, w_recv)

    def swap_gradient(q):
        def make(sender, send, recv):
            source, target = gradients.at[pl.ds(q * quarter, quarter)], gradients.at[pl.ds(rows + q * quarter, quarter)]
            return copy(source, target, send, recv, sibling)

        return make

    for q in range(4):
        here = slice(q * quarter, (q + 1) * quarter)
        pull = mine[Z - 1, here, :] + sib_in[Z - 1, here, :].astype(SINGLE)
        for s in (1, 0):
            run_copy(s, 3, q).wait_recv()
            pull = pull + run_in[s * 4 + 3, here, :].astype(SINGLE)
        gradients[here, :] = jnp.where(live[here, :] > 0.5, 0.5 * pull, 0.0).astype(HALF)
        terms.add(("c", q), swap_gradient(q))
        terms.start(("c", q))
    gradient = gradients[0:rows, :]

    embed_out[...] = gradient
    stores = [pltpu.make_async_copy(embed_out, grad_embed, store.at[0])]
    stores[0].start()
    gather.wait("feats")
    split = embed // 2
    share = group // XH

    side = 2 * share

    def first_copy(table, s, step, p):
        mate, size, at = (x_mate, X, x) if table == 0 else (y_mate, Y, y)
        near, far = (at + s + size) % size, (at + 2) % size
        low = s == 1
        way = 0 if s == 1 else 1
        stepped, plain = pl.ds((0 if low else side) + p * share, share), pl.ds(side if low else 0, side)

        def make(sender, send, recv):
            if step == 0:
                return copy(first_out.at[table, far, stepped], first_stop.at[table, way, pl.ds(p * share, share)], send, recv, mate(s))
            rows_of = plain if step == 1 else stepped
            return copy(first_out.at[table, near, rows_of], first_in.at[table, way, rows_of], send, recv, mate(s))

        return make

    def second(table, mate, size, at, d):
        def make(sender, send, recv):
            return copy(
                second_out.at[table, (at + d) % size],
                second_in.at[table, at if sender else (at - d + size) % size],
                send, recv, mate(d),
            )

        return make

    def third(d):
        def make(sender, send, recv):
            return copy(third_out.at[(z + d) % Z], third_in.at[z if sender else (z - d + Z) % Z], send, recv, z_mate(d))

        return make

    for table in (0, 1):
        for s in both:
            for step in range(3):
                for p in range(1 if step == 1 else 2):
                    terms.add(("first", table, s, step, p), first_copy(table, s, step, p))
    for d in range(1, X):
        terms.add(("second", 1, d), second(1, x_mate, X, x, d))
    for d in range(1, Y):
        terms.add(("second", 0, d), second(0, y_mate, Y, y, d))
    for d in range(1, Z):
        terms.add(("third", d), third(d))

    terms.wait(*[("c", q) for q in range(4)])
    both_gradients = gradients[...]
    for g in range(Y * XL):
        to_y, low = g // XL, g % XL
        term = (
            jnp.dot(turned[g * group : (g + 1) * group, :], both_gradients, preferred_element_type=SINGLE) * scale
        ).astype(HALF)
        for high in range(XH):
            to_x = high * XL + low
            piece = term[high * share : (high + 1) * share, :]
            first_out[0, to_x, to_y * share : (to_y + 1) * share, :] = piece[:, 0:split]
            first_out[1, to_y, to_x * share : (to_x + 1) * share, :] = piece[:, split:embed]
    for step, p in ((0, 0), (0, 1), (1, 0)):
        terms.start(*[("first", table, s, step, p) for table in (0, 1) for s in both])
    feats_out[...] = nt(gradient, weight[...]).astype(HALF)
    gather.finish()
    for n in range(Z):
        pair_copy(n).wait_send()
    for s in (0, 1):
        for m in range(4):
            for q in range(4):
                if comes(s, m, q):
                    run_copy(s, m, q).wait_send()
    stores.append(pltpu.make_async_copy(feats_out, grad_feats, store.at[1]))
    stores[1].start()
    for p, table, s in [(p, table, s) for p in (0, 1) for table in (0, 1) for s in both]:
        terms.wait(("first", table, s, 0, p))
        near, way = ((x if table == 0 else y) + s + 4) % 4, 0 if s == 1 else 1
        start = (0 if s == 1 else side) + p * share
        here = slice(start, start + share)
        passed = first_out[table, near, here].astype(SINGLE)
        passed = passed + first_stop[table, way, p * share : (p + 1) * share].astype(SINGLE)
        first_out[table, near, here] = passed.astype(HALF)
        terms.start(("first", table, s, 2, p))
    for table, at in ((0, x), (1, y)):
        terms.wait(*[("first", table, s, step, p) for s in both for step, p in ((1, 0), (2, 0), (2, 1))])
        added = first_out[table, at].astype(SINGLE)
        added = (added + first_in[table, 0].astype(SINGLE) + first_in[table, 1].astype(SINGLE)).astype(HALF)
        for i in range(4):
            second_out[table, i] = added[i * share : (i + 1) * share, :]
        terms.start(*[("second", table, d) for d in range(1, X)])
    totals = []
    for table, at in ((0, y), (1, x)):
        second_in[table, at] = second_out[table, at]
        terms.wait(*[("second", table, d) for d in range(1, X)])
        totals.append(jnp.sum(second_in[table].astype(SINGLE), axis=0))
    few = share // Z
    for i in range(Z):
        here = slice(i * few, (i + 1) * few)
        third_out[i] = jnp.concatenate([total[here, :] for total in totals], axis=0).astype(HALF)
    terms.start(*[("third", d) for d in range(1, Z)])
    third_in[z] = third_out[z]
    terms.wait(*terms.made)
    summed = jnp.sum(third_in[...].astype(SINGLE), axis=0)
    weight_out[...] = jnp.concatenate([summed[0:few, :], summed[few : 2 * few, :]], axis=1)
    stores.append(pltpu.make_async_copy(weight_out, grad_weight, store.at[2]))
    stores[2].start()

    terms.finish()
    for one in stores:
        one.wait()


def place(*refs):
    sources, targets, held, get, put = refs[0:3], refs[3:6], refs[6:9], refs[9], refs[10]
    gets = [pltpu.make_async_copy(a, b, get.at[i]) for i, (a, b) in enumerate(zip(sources, held))]
    puts = [pltpu.make_async_copy(a, b, put.at[i]) for i, (a, b) in enumerate(zip(held, targets))]
    for one in gets:
        one.start()
    for one, other in zip(gets, puts):
        one.wait()
        other.start()
    for one in puts:
        one.wait()


def local(feats, weight, valid):
    rows, width = feats.shape
    embed = weight.shape[1]
    frames = rows * LINE * PLANE
    out_rows = width // (LINE * PLANE)
    hbm = pl.BlockSpec(memory_space=pl.ANY)

    def half(*shape):
        return pltpu.VMEM(shape, HALF)

    def single(*shape):
        return pltpu.VMEM(shape, SINGLE)

    def dma(n):
        return [pltpu.SemaphoreType.DMA((n,))] * 2

    share = Z * out_rows
    columns = PLANE * rows
    shapes = (
        jax.ShapeDtypeStruct((rows, embed), HALF),
        jax.ShapeDtypeStruct((rows, width), HALF),
        jax.ShapeDtypeStruct((out_rows, embed), SINGLE),
    )
    results = pl.pallas_call(
        functools.partial(kernel, band=float(embed // 4), scale=math.sqrt(width) / frames),
        out_shape=shapes,
        in_specs=[hbm] * 3,
        out_specs=(hbm,) * 3,
        scratch_shapes=[
            half(rows, width), half(width, embed), pltpu.VMEM((1, rows), jnp.int32),
            half(rows, embed), half(rows, width), single(out_rows, embed),
            half(LINE * rows, embed), half(columns, embed), half(embed, columns), single(1, columns), single(LINE * rows, columns),
            single(LINE * rows, 128), single(LINE * rows, 128), single(8, columns),
            single(Z, C * rows), single(Z, C * rows), single(Z, C * rows), single(Z, Z, C * rows),
            single(1, columns), single(X, 1, columns), single(1, columns), single(Y, 1, columns),
            single(Z, rows, embed), half(Z, rows, embed), half(Z, rows, embed),
            half(8, rows, embed), half(8, rows, embed),
            half(2 * rows, width // 2), half(rows, width // 2), half(width // 2, 2 * rows), half(2 * rows, embed),
            half(2, 4, 4 * share, embed // 2), half(2, 2, 2 * share, embed // 2), half(2, 2, 4 * share, embed // 2),
            half(2, 4, share, embed // 2), half(2, 4, share, embed // 2),
            half(Z, 2 * out_rows, embed // 2), half(Z, 2 * out_rows, embed // 2),
        ]
        + [pltpu.SemaphoreType.DMA((6,)), pltpu.SemaphoreType.DMA((3,))]
        + dma(80) + dma(14) + dma(Z) + dma(32) + dma(37),
        compiler_params=pltpu.CompilerParams(
            collective_id=0, has_side_effects=True, vmem_limit_bytes=56 * 1024 * 1024
        ),
    )(feats, weight, valid.reshape(1, rows))
    return pl.pallas_call(
        place,
        out_shape=shapes,
        in_specs=[hbm] * 3,
        out_specs=(hbm,) * 3,
        scratch_shapes=[pltpu.VMEM(one.shape, one.dtype) for one in shapes] + dma(3),
    )(*results)


def solution(mesh):
    spec = P(("row", "col"), None)
    return jax.shard_map(
        local,
        mesh=mesh,
        in_specs=(spec, P(), P(("row", "col"))),
        out_specs=(spec, spec, spec),
        check_vma=False,
    )
```

```python
import functools
import math

import jax
import jax.numpy as jnp
from jax import lax
from jax.experimental import pallas as pl
from jax.experimental.pallas import tpu as pltpu
from jax.sharding import PartitionSpec as P

MESH = pl.DeviceIdType.MESH
XH, XL, Y, Z, C = 2, 2, 4, 8, 2
X = XH * XL
LINE = Z * C
PLANE = X * Y
FAR = 2.0**60
FARTHEST = (4, 3, 5, 2, 6, 1, 7)
ALONG = (0, 1, -1, 2, -2, 3, -3, 4)
AROUND = (
    (0, 0), (1, 0), (-1, 0), (0, 1), (0, -1), (2, 0), (0, 2), (1, 1), (-1, 1), (1, -1), (-1, -1),
    (2, 1), (2, -1), (1, 2), (-1, 2), (2, 2),
)
HALF, SINGLE = jnp.bfloat16, jnp.float32


def line_slot(dz):
    return ALONG.index((dz + Z // 2 - 1) % Z - Z // 2 + 1)


def plane_slot(dx, dy):
    return AROUND.index(((dx + 1) % X - 1, (dy + 1) % Y - 1))


def device(x, y, z, k):
    return {"row": (y * XL + x % XL) * C + k, "col": (x // XL) * Z + z}


def to_row(column):
    n = column.shape[0]
    eye = lax.broadcasted_iota(jnp.int32, (n, n), 0) == lax.broadcasted_iota(jnp.int32, (n, n), 1)
    return jnp.sum(jnp.where(eye, column, 0.0), axis=0, keepdims=True)


def to_column(row):
    n = row.shape[1]
    eye = lax.broadcasted_iota(jnp.int32, (n, n), 0) == lax.broadcasted_iota(jnp.int32, (n, n), 1)
    return jnp.sum(jnp.where(eye, row, 0.0), axis=1, keepdims=True)


def nt(a, b):
    return lax.dot_general(a, b, (((1,), (1,)), ((), ())), preferred_element_type=SINGLE)


def tn(a, b):
    return lax.dot_general(a, b, (((0,), (0,)), ((), ())), preferred_element_type=SINGLE)


class Gather:
    def __init__(self, send, recv):
        self.send, self.recv = send, recv
        self.made, self.arrived = {}, set()

    def add(self, name, make, needs=()):
        number = len(self.made)
        self.made[name] = (lambda mine: make(mine, self.send.at[number], self.recv.at[number])), needs

    def start(self, *names):
        for name in names:
            make, needs = self.made[name]
            for need in needs:
                self.wait(need)
            make(True).start()

    def wait(self, *names):
        for name in names:
            if name not in self.arrived:
                self.arrived.add(name)
                self.made[name][0](False).wait_recv()

    def finish(self):
        for name in self.made:
            self.made[name][0](True).wait_send()


def kernel(
    feats_in, weight_in, valid_in,
    grad_embed, grad_feats, grad_weight,
    feats, weight, valid, embed_out, feats_out, weight_out,
    lines, planes, planes_t, norms, tile, row_norm, row_sum, col_sum,
    row_mass, row_in, row_pair, row_ins, col_mass, col_ins, col_part, col_ins2,
    mine, sib_out, sib_in, run_out, run_in,
    mixed, leaving, turned, gradients, first_out, first_stop, first_in, second_out, second_in, third_out, third_in,
    load, store, g_send, g_recv, m_send, m_recv, s_send, s_recv, r_send, r_recv, w_send, w_recv,
    *, band, scale,
):
    rows, embed = grad_embed.shape
    r, c = lax.axis_index("row"), lax.axis_index("col")
    k, x, y, z = r % C, (c // Z) * XL + (r // C) % XL, r // (C * XL), c % Z
    sibling = device(x, y, z, 1 - k)

    def z_mate(d):
        return device(x, y, (z + d + Z) % Z, k)

    def x_mate(d):
        return device((x + d + X) % X, y, z, k)

    def y_mate(d):
        return device(x, (y + d + Y) % Y, z, k)

    barrier = pltpu.get_barrier_semaphore()
    friends = [sibling] + [z_mate(d) for d in range(1, Z)]
    friends += [x_mate(d) for d in range(1, X)] + [y_mate(d) for d in range(1, Y)]
    for friend in friends:
        pl.semaphore_signal(barrier, inc=1, device_id=friend, device_id_type=MESH)

    depth = weight.shape[0] // 4
    loads = [
        pltpu.make_async_copy(valid_in, valid, load.at[0]),
        pltpu.make_async_copy(feats_in, feats, load.at[1]),
    ]
    for i in range(4):
        part = pl.ds(i * depth, depth)
        loads.append(pltpu.make_async_copy(weight_in.at[part], weight.at[part], load.at[2 + i]))
    for one in loads:
        one.start()
    loads[0].wait()
    loads[1].wait()

    def span(start, n):
        return pl.ds(pl.multiple_of(start, n), n)

    def copy(src, dst, send, recv, target):
        return pltpu.make_async_remote_copy(
            src_ref=src, dst_ref=dst, send_sem=send, recv_sem=recv, device_id=target, device_id_type=MESH
        )

    live = to_column(jnp.where(valid[...] > 0, 1.0, 0.0))
    embedding = jnp.zeros((rows, embed), SINGLE)
    for i in range(4):
        loads[2 + i].wait()
        part = slice(i * depth, (i + 1) * depth)
        embedding = embedding + jnp.dot(feats[:, part], weight[part, :], preferred_element_type=SINGLE)
    away = jnp.where(lax.broadcasted_iota(jnp.int32, (rows, embed), 1) == 0, FAR, 0.0)
    own = jnp.where(live > 0.5, embedding, away).astype(HALF)
    lines[span(k * rows, rows), :] = own
    planes[0:rows, :] = own
    pl.semaphore_wait(barrier, len(friends))

    half, quarter = rows // 2, rows // 4
    gather = Gather(g_send, g_recv)

    def line_at(dz, core, start, n):
        return lines.at[span((line_slot(dz) * C + core) * rows + start, n)]

    def plane_at(dx, dy, start, n):
        return planes.at[pl.ds(plane_slot(dx, dy) * rows + start, n)]

    def along_z(s, d, q):
        at = (q if s == 1 else 3 - q) * quarter

        def make(sender, send, recv):
            source = line_at(-s * (d - 1), k, at, quarter)
            return copy(source, line_at(-s * d, k, at, quarter), send, recv, z_mate(s))

        return make

    for s in (1, -1):
        for d in range(1, Z // 2 + 1):
            for q in range(4 if d < Z // 2 else 2):
                gather.add(("z", s, d, q), along_z(s, d, q), [("z", s, d - 1, q)] if d > 1 else [])

    def across(o):
        def make(sender, send, recv):
            ref = line_at(o, k if sender else 1 - k, 0, rows)
            return copy(ref, ref, send, recv, sibling)

        return make

    for o in range(-Z // 2 + 1, Z // 2 + 1):
        if o == 0:
            needs = []
        elif o == Z // 2:
            needs = [("z", s, o, q) for s in (1, -1) for q in (0, 1)]
        else:
            needs = [("z", -1 if o > 0 else 1, abs(o), q) for q in range(4)]
        gather.add(("c", o), across(o), needs)

    def in_plane(axis, s, along, beside, start, n):
        def make(sender, send, recv):
            if axis == "x":
                source, target = plane_at(along, beside, start, n), plane_at(along - s, beside, start, n)
                return copy(source, target, send, recv, x_mate(s))
            source, target = plane_at(beside, along, start, n), plane_at(beside, along - s, start, n)
            return copy(source, target, send, recv, y_mate(s))

        return make

    for axis, other, h in (("y", "x", 0), ("x", "y", 1)):
        for s in (1, -1):
            part = 0 if s == 1 else 1
            for g in (0, 1):
                gather.add((axis, s, "own", g), in_plane(axis, s, 0, 0, g * half, half))
            gather.add((axis, s, "far"), in_plane(axis, s, -s, 0, part * half, half), [(axis, s, "own", part)])
            for t in (1, -1):
                gather.add((axis, s, "side", t), in_plane(axis, s, 0, t, h * half, half), [(other, -t, "own", h)])
                gather.add(
                    (axis, s, "side far", t),
                    in_plane(axis, s, -s, t, h * half + part * quarter, quarter),
                    [(axis, s, "side", t)],
                )
            gather.add(
                (axis, s, "across"),
                in_plane(axis, s, 0, 2, h * half, half),
                [(other, 1 if h == 0 else -1, "far")],
            )
            gather.add(
                (axis, s, "across far"),
                in_plane(axis, s, -s, 2, h * half + part * quarter, quarter),
                [(axis, s, "across")],
            )

    def swap_copy(mine_, send, recv):
        return copy(leaving, mixed.at[span(rows, rows)], send, recv, sibling)

    gather.add("feats", swap_copy)

    both = (1, -1)
    def pass_z(d, *pieces):
        gather.start(*[("z", s, d, q) for q in pieces for s in both])

    gather.start(*[("x", s, "own", 0) for s in both], *[("y", s, "own", 1) for s in both])
    pass_z(1, 0, 1)
    gather.start(*[("x", s, "own", 1) for s in both], *[("y", s, "own", 0) for s in both])
    pass_z(1, 2, 3)
    gather.start(("c", 0))

    group = XH * Z * grad_weight.shape[0]
    for g in range(Y * XL):
        low, high = feats[:, 2 * g * group : (2 * g + 1) * group], feats[:, (2 * g + 1) * group : (2 * g + 2) * group]
        here = slice(g * group, (g + 1) * group)
        mixed[0:rows, here] = jnp.where(k == 0, low, high)
        leaving[:, here] = jnp.where(k == 0, high, low)
    gather.start("feats")

    def norm_of(first, last):
        for i in range(first, last):
            here = slice(i * rows, (i + 1) * rows)
            planes_t[:, here] = planes[here, :].T
            wide = planes[here, :].astype(SINGLE)
            norms[0:1, here] = to_row(jnp.sum(wide * wide, axis=1, keepdims=True))

    chunk = C * rows
    rate = -1.0 / (band * math.log(2.0))

    def work(first_row, last_row, first_unit, last_unit):
        def step(i, carry):
            here = span(i * chunk, chunk)
            block = lines[here, :]
            if first_unit == 0:
                wide = block.astype(SINGLE)
                norm = jnp.broadcast_to(jnp.sum(wide * wide, axis=1, keepdims=True), (chunk, 128))
                row_norm[here, :] = norm
                total = jnp.zeros((chunk, 128), SINGLE)
            else:
                norm = row_norm[here, :]
                total = row_sum[here, :]
            norm = jnp.concatenate([norm] * (chunk // 128), axis=1)
            twice = block * 2
            for j in range(first_unit, last_unit):
                there = slice(j * chunk, (j + 1) * chunk)
                distance = (norm + norms[0:1, there]) - jnp.dot(
                    twice, planes_t[:, there], preferred_element_type=SINGLE
                )
                value = jnp.exp2(distance * rate)
                tile[here, there] = value
                for p in range(chunk // 128):
                    total = total + value[:, p * 128 : (p + 1) * 128]
                col_sum[:, there] += jnp.sum(value.reshape(chunk // 8, 8, chunk), axis=0)
            row_sum[here, :] = total
            return carry

        lax.fori_loop(first_row, last_row, step, 0)

    col_sum[...] = jnp.zeros_like(col_sum)
    norm_of(0, 1)
    pass_z(2, 0)
    gather.start(("x", 1, "far"), ("y", -1, "far"))
    gather.start(*[(axis, s, "side", t) for t in both for axis in "yx" for s in both])
    pass_z(2, 1, 2, 3)
    gather.start(("x", -1, "far"), ("y", 1, "far"), ("c", 1), ("c", -1))
    gather.wait(*[(axis, s, "own", g) for axis in "xy" for s in both for g in (0, 1)])
    norm_of(1, 5)
    pass_z(3, 0, 1)
    gather.wait(("c", 0), ("c", 1), ("c", -1))
    work(0, 3, 0, 2)
    pass_z(3, 2, 3)
    gather.start(("c", 2), ("c", -2))
    gather.start(*[(axis, s, "across") for axis in "yx" for s in both])
    pass_z(4, 0, 1)
    gather.start(*[(axis, s, "side far", t) for t in both for axis in "yx" for s in both])
    gather.wait(*[(axis, s, "far") for axis in "xy" for s in both])
    norm_of(5, 11)
    work(0, 3, 2, 5)
    gather.start(*[(axis, s, "across far") for axis in "yx" for s in both])
    gather.start(("c", 3), ("c", -3), ("c", 4))
    gather.wait(("c", 2), ("c", -2))
    work(3, 5, 0, 5)
    gather.wait(*[(axis, s, "side far", t) for t in both for axis in "yx" for s in both])
    norm_of(11, 15)
    work(0, 5, 5, 7)
    gather.wait(("c", 3), ("c", -3))
    work(5, 7, 0, 7)
    gather.wait(*[(axis, s, "across far") for axis in "xy" for s in both])
    norm_of(15, 16)
    work(0, 7, 7, 8)
    gather.wait(*gather.made)
    work(7, 8, 0, 8)

    def absolute(slot):
        dx, dy = AROUND[slot]
        return span(((y + dy + Y) % Y * X + (x + dx + X) % X) * rows, rows)

    column_total = jnp.sum(col_sum[...], axis=0, keepdims=True)
    for i in range(PLANE):
        col_mass[0:1, absolute(i)] = column_total[:, i * rows : (i + 1) * rows]

    mass = Gather(m_send, m_recv)
    mass.add("c", lambda mine_, send, recv: copy(row_mass, row_in, send, recv, sibling))

    def direct(source, target, mate, size, at, d):
        def make(sender, send, recv):
            return copy(source, target.at[at if sender else (at - d + size) % size], send, recv, mate(d))

        return make

    for d in range(1, X):
        mass.add(("x", d), direct(col_mass, col_ins, x_mate, X, x, d))
    for d in range(1, Y):
        mass.add(("y", d), direct(col_part, col_ins2, y_mate, Y, y, d))
    for d in range(1, Z):
        mass.add(("z", d), direct(row_pair, row_ins, z_mate, Z, z, d))
    mass.start(*[("x", d) for d in (2, 1, 3)])
    col_ins[x] = col_mass[...]

    def row_total(i, carry):
        place = (z + (i + 1) // 2 * (2 * (i % 2) - 1) + Z) % Z
        row_mass[pl.ds(place, 1), :] = to_row(jnp.sum(row_sum[span(i * chunk, chunk), :], axis=1, keepdims=True))
        return carry

    lax.fori_loop(0, Z, row_total, 0)
    mass.start("c")
    for g in range(Y * XL):
        here = slice(g * group, (g + 1) * group)
        turned[here, :] = mixed[:, here].T
    mass.wait("c")
    row_pair[...] = row_mass[...] + row_in[...]
    mass.start(*[("z", d) for d in FARTHEST])
    row_ins[z] = row_pair[...]
    mass.wait(*[("x", d) for d in range(1, X)])
    col_part[...] = jnp.sum(col_ins[...], axis=0)
    mass.start(*[("y", d) for d in (2, 1, 3)])
    col_ins2[y] = col_part[...]
    mass.wait(*mass.made)
    mass.finish()
    row_mass[...] = 1.0 / jnp.sum(row_ins[...], axis=0)
    col_mass[...] = 1.0 / jnp.sum(col_ins2[...], axis=0)
    for i in range(PLANE):
        col_part[0:1, i * rows : (i + 1) * rows] = col_mass[0:1, absolute(i)]

    def pair_copy(n):
        return copy(sib_out.at[n], sib_in.at[n], s_send.at[n], s_recv.at[n], sibling)

    def run_copy(s, m, q):
        here = pl.ds(q * quarter, quarter)
        at = (s * 4 + m) * 4 + q
        return copy(
            run_out.at[s * 4 + m, here], run_in.at[s * 4 + m, here], r_send.at[at], r_recv.at[at], z_mate(2 * s - 1)
        )

    def comes(s, m, q):
        return m > 0 or q // 2 == 1 - s

    def link(m):
        for s in (0, 1):
            pair_copy(2 * m + 1 + s).wait_recv()
        for q in range(4):
            here = slice(q * quarter, (q + 1) * quarter)
            for s in (1, 0):
                n = 2 * m + 1 + s
                total = mine[n, here, :] + sib_in[n, here, :].astype(SINGLE)
                if comes(s, m, q):
                    run_copy(s, m, q).wait_recv()
                    total = total + run_in[s * 4 + m, here, :].astype(SINGLE)
                run_out[s * 4 + m + 1, here, :] = total.astype(HALF)
                run_copy(s, m + 1, q).start()

    def pull_step(n, carry):
        j = Z - 1 - n
        i = (z + (j + 1) // 2 * (2 * (j % 2) - 1) + Z) % Z
        here = span(j * chunk, chunk)
        inverse = to_column(row_mass[pl.ds(i, 1), :])
        total = jnp.zeros((chunk, 1), SINGLE)
        moved = jnp.zeros((chunk, embed), SINGLE)
        width = 2 * chunk
        for j in range(PLANE * rows // width):
            there = slice(j * width, (j + 1) * width)
            pair = ((inverse + col_part[0:1, there]) * tile[here, there]).astype(HALF)
            total = total + jnp.sum(pair.astype(SINGLE), axis=1, keepdims=True)
            moved = moved + jnp.dot(pair, planes[there, :], preferred_element_type=SINGLE)
        pull = lines[here, :].astype(SINGLE) * total - moved
        mine[n] = jnp.where(k == 0, pull[0:rows, :], pull[rows:chunk, :])
        sib_out[n] = jnp.where(k == 0, pull[rows:chunk, :], pull[0:rows, :]).astype(HALF)
        pair_copy(n).start()

        @pl.when(n == 1)
        def _():
            pair_copy(0).wait_recv()
            far = (mine[0] + sib_in[0].astype(SINGLE)).astype(HALF)
            run_out[4] = far
            run_out[0] = far
            for q in range(4):
                run_copy(1 - q // 2, 0, q).start()

        for m, after in ((0, 3), (1, 6), (2, 7)):

            @pl.when(n == after)
            def _():
                link(m)

        return carry

    lax.fori_loop(0, Z, pull_step, 0)
    pair_copy(Z - 1).wait_recv()
    terms = Gather(w_send, w_recv)

    def swap_gradient(q):
        def make(sender, send, recv):
            source, target = gradients.at[pl.ds(q * quarter, quarter)], gradients.at[pl.ds(rows + q * quarter, quarter)]
            return copy(source, target, send, recv, sibling)

        return make

    for q in range(4):
        here = slice(q * quarter, (q + 1) * quarter)
        pull = mine[Z - 1, here, :] + sib_in[Z - 1, here, :].astype(SINGLE)
        for s in (1, 0):
            run_copy(s, 3, q).wait_recv()
            pull = pull + run_in[s * 4 + 3, here, :].astype(SINGLE)
        gradients[here, :] = jnp.where(live[here, :] > 0.5, 0.5 * pull, 0.0).astype(HALF)
        terms.add(("c", q), swap_gradient(q))
        terms.start(("c", q))
    gradient = gradients[0:rows, :]

    embed_out[...] = gradient
    stores = [pltpu.make_async_copy(embed_out, grad_embed, store.at[0])]
    stores[0].start()
    gather.wait("feats")
    split = embed // 2
    share = group // XH

    side = 2 * share

    def first_copy(table, s, step, p):
        mate, size, at = (x_mate, X, x) if table == 0 else (y_mate, Y, y)
        near, far = (at + s + size) % size, (at + 2) % size
        low = s == 1
        way = 0 if s == 1 else 1
        stepped, plain = pl.ds((0 if low else side) + p * share, share), pl.ds(side if low else 0, side)

        def make(sender, send, recv):
            if step == 0:
                return copy(first_out.at[table, far, stepped], first_stop.at[table, way, pl.ds(p * share, share)], send, recv, mate(s))
            rows_of = plain if step == 1 else stepped
            return copy(first_out.at[table, near, rows_of], first_in.at[table, way, rows_of], send, recv, mate(s))

        return make

    def second(table, mate, size, at, d):
        def make(sender, send, recv):
            return copy(
                second_out.at[table, (at + d) % size],
                second_in.at[table, at if sender else (at - d + size) % size],
                send, recv, mate(d),
            )

        return make

    def third(d):
        def make(sender, send, recv):
            return copy(third_out.at[(z + d) % Z], third_in.at[z if sender else (z - d + Z) % Z], send, recv, z_mate(d))

        return make

    for table in (0, 1):
        for s in both:
            for step in range(3):
                for p in range(1 if step == 1 else 2):
                    terms.add(("first", table, s, step, p), first_copy(table, s, step, p))
    for d in range(1, X):
        terms.add(("second", 1, d), second(1, x_mate, X, x, d))
    for d in range(1, Y):
        terms.add(("second", 0, d), second(0, y_mate, Y, y, d))
    for d in range(1, Z):
        terms.add(("third", d), third(d))

    terms.wait(*[("c", q) for q in range(4)])
    both_gradients = gradients[...]
    for g in range(Y * XL):
        to_y, low = g // XL, g % XL
        term = (
            jnp.dot(turned[g * group : (g + 1) * group, :], both_gradients, preferred_element_type=SINGLE) * scale
        ).astype(HALF)
        for high in range(XH):
            to_x = high * XL + low
            piece = term[high * share : (high + 1) * share, :]
            first_out[0, to_x, to_y * share : (to_y + 1) * share, :] = piece[:, 0:split]
            first_out[1, to_y, to_x * share : (to_x + 1) * share, :] = piece[:, split:embed]
    for step, p in ((0, 0), (0, 1), (1, 0)):
        terms.start(*[("first", table, s, step, p) for table in (0, 1) for s in both])
    feats_out[...] = nt(gradient, weight[...]).astype(HALF)
    gather.finish()
    for n in range(Z):
        pair_copy(n).wait_send()
    for s in (0, 1):
        for m in range(4):
            for q in range(4):
                if comes(s, m, q):
                    run_copy(s, m, q).wait_send()
    stores.append(pltpu.make_async_copy(feats_out, grad_feats, store.at[1]))
    stores[1].start()
    for p, table, s in [(p, table, s) for p in (0, 1) for table in (0, 1) for s in both]:
        terms.wait(("first", table, s, 0, p))
        near, way = ((x if table == 0 else y) + s + 4) % 4, 0 if s == 1 else 1
        start = (0 if s == 1 else side) + p * share
        here = slice(start, start + share)
        passed = first_out[table, near, here].astype(SINGLE)
        passed = passed + first_stop[table, way, p * share : (p + 1) * share].astype(SINGLE)
        first_out[table, near, here] = passed.astype(HALF)
        terms.start(("first", table, s, 2, p))
    for table, at in ((0, x), (1, y)):
        terms.wait(*[("first", table, s, step, p) for s in both for step, p in ((1, 0), (2, 0), (2, 1))])
        added = first_out[table, at].astype(SINGLE)
        added = (added + first_in[table, 0].astype(SINGLE) + first_in[table, 1].astype(SINGLE)).astype(HALF)
        for i in range(4):
            second_out[table, i] = added[i * share : (i + 1) * share, :]
        terms.start(*[("second", table, d) for d in (2, 1, 3)])
    totals = []
    for table, at in ((0, y), (1, x)):
        second_in[table, at] = second_out[table, at]
        terms.wait(*[("second", table, d) for d in range(1, X)])
        totals.append(jnp.sum(second_in[table].astype(SINGLE), axis=0))
    few = share // Z
    for i in range(Z):
        here = slice(i * few, (i + 1) * few)
        third_out[i] = jnp.concatenate([total[here, :] for total in totals], axis=0).astype(HALF)
    terms.start(*[("third", d) for d in FARTHEST])
    third_in[z] = third_out[z]
    terms.wait(*terms.made)
    summed = jnp.sum(third_in[...].astype(SINGLE), axis=0)
    weight_out[...] = jnp.concatenate([summed[0:few, :], summed[few : 2 * few, :]], axis=1)
    stores.append(pltpu.make_async_copy(weight_out, grad_weight, store.at[2]))
    stores[2].start()

    terms.finish()
    for one in stores:
        one.wait()


def place(*refs):
    sources, targets, held, get, put = refs[0:3], refs[3:6], refs[6:9], refs[9], refs[10]
    gets = [pltpu.make_async_copy(a, b, get.at[i]) for i, (a, b) in enumerate(zip(sources, held))]
    puts = [pltpu.make_async_copy(a, b, put.at[i]) for i, (a, b) in enumerate(zip(held, targets))]
    for one in gets:
        one.start()
    for one, other in zip(gets, puts):
        one.wait()
        other.start()
    for one in puts:
        one.wait()


def local(feats, weight, valid):
    rows, width = feats.shape
    embed = weight.shape[1]
    frames = rows * LINE * PLANE
    out_rows = width // (LINE * PLANE)
    hbm = pl.BlockSpec(memory_space=pl.ANY)

    def half(*shape):
        return pltpu.VMEM(shape, HALF)

    def single(*shape):
        return pltpu.VMEM(shape, SINGLE)

    def dma(n):
        return [pltpu.SemaphoreType.DMA((n,))] * 2

    share = Z * out_rows
    columns = PLANE * rows
    shapes = (
        jax.ShapeDtypeStruct((rows, embed), HALF),
        jax.ShapeDtypeStruct((rows, width), HALF),
        jax.ShapeDtypeStruct((out_rows, embed), SINGLE),
    )
    results = pl.pallas_call(
        functools.partial(kernel, band=float(embed // 4), scale=math.sqrt(width) / frames),
        out_shape=shapes,
        in_specs=[hbm] * 3,
        out_specs=(hbm,) * 3,
        scratch_shapes=[
            half(rows, width), half(width, embed), pltpu.VMEM((1, rows), jnp.int32),
            half(rows, embed), half(rows, width), single(out_rows, embed),
            half(LINE * rows, embed), half(columns, embed), half(embed, columns), single(1, columns), single(LINE * rows, columns),
            single(LINE * rows, 128), single(LINE * rows, 128), single(8, columns),
            single(Z, C * rows), single(Z, C * rows), single(Z, C * rows), single(Z, Z, C * rows),
            single(1, columns), single(X, 1, columns), single(1, columns), single(Y, 1, columns),
            single(Z, rows, embed), half(Z, rows, embed), half(Z, rows, embed),
            half(8, rows, embed), half(8, rows, embed),
            half(2 * rows, width // 2), half(rows, width // 2), half(width // 2, 2 * rows), half(2 * rows, embed),
            half(2, 4, 4 * share, embed // 2), half(2, 2, 2 * share, embed // 2), half(2, 2, 4 * share, embed // 2),
            half(2, 4, share, embed // 2), half(2, 4, share, embed // 2),
            half(Z, 2 * out_rows, embed // 2), half(Z, 2 * out_rows, embed // 2),
        ]
        + [pltpu.SemaphoreType.DMA((6,)), pltpu.SemaphoreType.DMA((3,))]
        + dma(80) + dma(14) + dma(Z) + dma(32) + dma(37),
        compiler_params=pltpu.CompilerParams(
            collective_id=0, has_side_effects=True, vmem_limit_bytes=56 * 1024 * 1024
        ),
    )(feats, weight, valid.reshape(1, rows))
    return pl.pallas_call(
        place,
        out_shape=shapes,
        in_specs=[hbm] * 3,
        out_specs=(hbm,) * 3,
        scratch_shapes=[pltpu.VMEM(one.shape, one.dtype) for one in shapes] + dma(3),
    )(*results)


def solution(mesh):
    spec = P(("row", "col"), None)
    return jax.shard_map(
        local,
        mesh=mesh,
        in_specs=(spec, P(), P(("row", "col"))),
        out_specs=(spec, spec, spec),
        check_vma=False,
    )
```
